128 devices in a mesh: ctx: 16 (over z, x_hi, core), head: 8 (over y, x_lo).
Axes of the slice: x: 4 (x_hi: 2, x_lo: 2; x = x_hi * 2 + x_lo), y: 4, z: 4, core: 2. Of those that a mesh axis runs over, the one named last changes fastest.
Arguments:
- queries: bfloat16 [2048, 8192], P('ctx', 'head'), may hold values from -17.5 to 17.5
- incoming_keys: bfloat16 [2048, 1024], P('ctx', 'head'), may hold values from -7.5 to 7.5
- incoming_values: bfloat16 [2048, 1024], P('ctx', 'head'), may hold values from -6 to 6
- paged_key_cache: bfloat16 [256, 8, 128, 128], P('ctx', 'head'), may hold values from -7.5 to 7.5
- paged_value_cache: bfloat16 [256, 8, 128, 128], P('ctx', 'head'), may hold values from -6 to 6
- block_table: int32 [4, 64], replicated, may hold values from 0 to 255, as said below
- cache_len: int32 [4], replicated, may hold values from 2048 to 8192
- new_start: int32 [5], replicated, may hold values from 0 to 2048, as said below
- out_weight: bfloat16 [8192, 8192], P('head'), may hold values from -0.09375 to 0.09375
Outputs:
- mixed: bfloat16 [2048, 8192], P('ctx', 'head')
The draws below stay inside these ranges and needn't reach their ends.
Inputs may be any that keep to these rules, and one draw needn't show every extreme that they name: `block_table`: each page slot appears exactly once; row r lists the page slots of request r's pages in order. Rises strictly from new_start[0] = 0 to new_start[4] = 2048.
All inputs are finite; a program needn't handle non-finite values.
Results may differ from the reference program's by a relative error of at most 0.0055.
Values may be sent and summed in bfloat16 or wider, within the bound.
No kernel may reach another device: no remote copies, remote signals or barrier semaphores. Data moves between devices by JAX's collectives and lax.ppermute only.
A program may use at most 128 MiB of HBM per device.

```python
import math
import jax
import jax.numpy as jnp
from jax import lax

D = 8192
QUERY_HEADS = 64
KEY_VALUE_HEADS = 8
HEAD_SIZE = 128
PAGE_TOKENS = 128
REQS = 4
NEW_TOKEN_COUNT = 2048
PAGE_SLOTS = 256
MAXP = 64


def table_order(key):
    return jax.random.permutation(jax.random.fold_in(key, 21), PAGE_SLOTS).astype(jnp.int32)


def draw_queries(key, part):
    key = jax.random.fold_in(key, 11)
    value_rows = jnp.clip(jax.random.normal(key, (NEW_TOKEN_COUNT, QUERY_HEADS, HEAD_SIZE), jnp.float32), -4.0, 4.0)
    return value_rows.reshape(NEW_TOKEN_COUNT, QUERY_HEADS * HEAD_SIZE).astype(jnp.bfloat16)


def draw_incoming_keys(key, part):
    key = jax.random.fold_in(key, 13)
    value_rows = jnp.clip(jax.random.normal(key, (NEW_TOKEN_COUNT, KEY_VALUE_HEADS, HEAD_SIZE), jnp.float32), -4.0, 4.0)
    return value_rows.reshape(NEW_TOKEN_COUNT, KEY_VALUE_HEADS * HEAD_SIZE).astype(jnp.bfloat16)


def draw_paged_key_cache(key, part):
    key = jax.random.fold_in(key, 12)
    value_rows = jnp.clip(jax.random.normal(key, (PAGE_SLOTS, KEY_VALUE_HEADS, PAGE_TOKENS, HEAD_SIZE), jnp.float32), -4.0, 4.0)
    return value_rows.astype(jnp.bfloat16)


def draw_block_table(key, part):
    order = table_order(key)
    return order.reshape(REQS, MAXP)


def draw_cache_len(key, part):
    key = jax.random.fold_in(key, 22)
    first_key, second_key = jax.random.split(key)
    lengths = jax.random.randint(first_key, (REQS,), MAXP * PAGE_TOKENS // 4, MAXP * PAGE_TOKENS + 1)
    longest = jax.random.randint(second_key, (), 0, REQS)
    return jnp.where(jnp.arange(REQS) == longest, MAXP * PAGE_TOKENS, lengths).astype(jnp.int32)


def draw_new_start(key, part):
    key = jax.random.fold_in(key, 23)
    cuts = jnp.sort(jax.random.permutation(key, NEW_TOKEN_COUNT - 1)[:REQS - 1] + 1)
    return jnp.concatenate([jnp.zeros((1,), jnp.int32), cuts.astype(jnp.int32), jnp.full((1,), NEW_TOKEN_COUNT, jnp.int32)])


def with_spikes(result, stream_key, source, target, blocks, factor):
    def block_of(dim):
        return (jnp.arange(result.shape[dim]) // (result.shape[dim] // blocks)).reshape((-1,) + (1,) * (result.ndim - 1 - dim))

    near = jax.random.permutation(stream_key, blocks)[block_of(target)]
    other_side = (block_of(target) + blocks // 2) % blocks
    return jnp.where((block_of(source) == near) | (block_of(source) == other_side), factor * result, result)


def shard_levels(key, dims, pieces, smallest, high):
    level = 1.0
    for axis_at, shards_of in pieces:
        steps = jax.random.uniform(jax.random.fold_in(jax.random.fold_in(key, 6), axis_at), (shards_of,), jnp.float32, smallest / len(pieces), high / len(pieces))
        level = level * jnp.repeat(jnp.exp(steps), dims[axis_at] // shards_of).reshape((-1,) + (1,) * (len(dims) - 1 - axis_at))
    return level


def gaussian(stream_key, shape, spread, most, cuts=(), held_as=jnp.bfloat16):
    entries = spread * jax.random.normal(stream_key, shape, jnp.float32)
    if cuts:
        entries = entries * shard_levels(stream_key, shape, cuts, -0.22, 0.18)
    return jnp.clip(entries, -most, most).astype(held_as)


def gaussian_with(rng, shape, scale, reach, cuts, heavy, kind=jnp.bfloat16):
    drawn = scale * jax.random.normal(rng, shape, jnp.float32)
    if cuts:
        drawn = drawn * shard_levels(rng, shape, cuts, -0.22, 0.18)
    return jnp.clip(with_spikes(drawn, jax.random.fold_in(rng, 3), *heavy), -reach, reach).astype(kind)


def setup_inputs(seed: int = 0) -> dict:
    key_of = jax.random.split(jax.random.key(seed), 10)
    queries = draw_queries(jax.random.fold_in(key_of[9], 71), 0)
    incoming_keys = draw_incoming_keys(jax.random.fold_in(key_of[9], 71), 0)
    incoming_values = gaussian(key_of[2], (NEW_TOKEN_COUNT, KEY_VALUE_HEADS * HEAD_SIZE), 1.0, 6.0, ((0, 16), (1, 8)))
    paged_key_cache = draw_paged_key_cache(jax.random.fold_in(key_of[9], 71), 0)
    paged_value_cache = gaussian(key_of[4], (PAGE_SLOTS, KEY_VALUE_HEADS, PAGE_TOKENS, HEAD_SIZE), 1.0, 6.0, ((0, 16), (1, 8)))
    block_table = draw_block_table(jax.random.fold_in(key_of[9], 71), 0)
    cache_len = draw_cache_len(jax.random.fold_in(key_of[9], 71), 0)
    new_start = draw_new_start(jax.random.fold_in(key_of[9], 71), 0)
    out_weight = gaussian_with(key_of[8], (QUERY_HEADS * HEAD_SIZE, D), (QUERY_HEADS * HEAD_SIZE) ** -0.5, 0.09375, ((0, 8),), (0, 1, 8, 2.0))
    return {"queries": queries, "incoming_keys": incoming_keys, "incoming_values": incoming_values, "paged_key_cache": paged_key_cache, "paged_value_cache": paged_value_cache, "block_table": block_table, "cache_len": cache_len, "new_start": new_start, "out_weight": out_weight}


negative_fill = -1e+30

def token_meta(positions, cache_len, new_start):
    requests = cache_len.shape[0]
    owners = lax.optimization_barrier(jnp.sum((positions[:, None] >= new_start[None, 1:requests]).astype(jnp.int32), axis=1))
    onehot = (owners[:, None] == jnp.arange(requests, dtype=jnp.int32)[None, :]).astype(jnp.int32)
    shifted = lax.optimization_barrier(jnp.sum(onehot * (cache_len - new_start[:requests])[None, :], axis=1))
    return (owners, shifted + positions)

def slot_meta(slot_ids, block_table, cache_len, page_size):
    requests, most = block_table.shape
    match = (block_table[:, :, None] == slot_ids[None, None, :]).astype(jnp.int32)
    owners = lax.optimization_barrier(jnp.sum(match * jnp.arange(requests, dtype=jnp.int32)[:, None, None], axis=(0, 1)))
    page_index = lax.optimization_barrier(jnp.sum(match * jnp.arange(most, dtype=jnp.int32)[None, :, None], axis=(0, 1)))
    limits = lax.optimization_barrier(jnp.sum(match * cache_len[:, None, None], axis=(0, 1)))
    places = page_index[:, None] * page_size + jnp.arange(page_size, dtype=jnp.int32)[None, :]
    key_owner = jnp.broadcast_to(owners[:, None], places.shape)
    return (key_owner, places, places < limits[:, None])

def attend(head_queries, keys, value_rows, query_owner, query_place, key_owner, key_place, key_live, scale_factor):
    scores = jnp.einsum('qkgd,kbtd->kgqbt', head_queries.astype(jnp.float32), keys.astype(jnp.float32)) * scale_factor
    allowed = (query_owner[:, None, None] == key_owner[None]) & (key_place[None] <= query_place[:, None, None]) & key_live[None]
    masked = jnp.where(allowed, scores, negative_fill)
    block_high = lax.optimization_barrier(jnp.max(masked, axis=-1))
    weights = jnp.where(allowed, jnp.exp(masked - block_high[..., None]), 0.0)
    block_total = lax.optimization_barrier(jnp.sum(weights, axis=-1))
    rounded = lax.optimization_barrier(weights.astype(jnp.bfloat16))
    block_numer = jnp.einsum('kgqbt,kbtd->kgqbd', rounded.astype(jnp.float32), value_rows.astype(jnp.float32))
    highest = lax.optimization_barrier(jnp.max(block_high, axis=-1))
    scaled = jnp.exp(block_high - highest[..., None])
    return (highest, lax.optimization_barrier(jnp.sum(scaled * block_total, axis=-1)), lax.optimization_barrier(jnp.sum(scaled[..., None] * block_numer, axis=-2)))

def reference(queries, incoming_keys, incoming_values, paged_key_cache, paged_value_cache, block_table, cache_len, new_start, out_weight):
    query_group_width = QUERY_HEADS // KEY_VALUE_HEADS
    scale_factor = 1.0 / math.sqrt(HEAD_SIZE)
    positions = jnp.arange(NEW_TOKEN_COUNT, dtype=jnp.int32)
    token_owner, token_place = token_meta(positions, cache_len, new_start)
    cache_owner, cache_place, cache_live = slot_meta(jnp.arange(PAGE_SLOTS, dtype=jnp.int32), block_table, cache_len, PAGE_TOKENS)
    fresh_token_blocks = NEW_TOKEN_COUNT // PAGE_TOKENS
    key_owner = jnp.concatenate([cache_owner, token_owner.reshape(fresh_token_blocks, PAGE_TOKENS)], 0)
    key_place = jnp.concatenate([cache_place, token_place.reshape(fresh_token_blocks, PAGE_TOKENS)], 0)
    key_live = jnp.concatenate([cache_live, jnp.ones((fresh_token_blocks, PAGE_TOKENS), dtype=bool)], 0)
    joined_keys = jnp.concatenate([paged_key_cache, incoming_keys.reshape(fresh_token_blocks, PAGE_TOKENS, KEY_VALUE_HEADS, HEAD_SIZE).transpose(0, 2, 1, 3)], 0).transpose(1, 0, 2, 3)
    joined_values = jnp.concatenate([paged_value_cache, incoming_values.reshape(fresh_token_blocks, PAGE_TOKENS, KEY_VALUE_HEADS, HEAD_SIZE).transpose(0, 2, 1, 3)], 0).transpose(1, 0, 2, 3)
    grouped_query_blocks = queries.reshape(fresh_token_blocks, PAGE_TOKENS, KEY_VALUE_HEADS, query_group_width, HEAD_SIZE).transpose(0, 2, 1, 3, 4)
    owner_blocks = token_owner.reshape(fresh_token_blocks, PAGE_TOKENS)
    place_blocks = token_place.reshape(fresh_token_blocks, PAGE_TOKENS)

    def per_block(items):
        block_queries, owners, places = items

        def per_head(head_items):
            head_queries, head_keys, head_values = head_items
            highest, total, numer = attend(head_queries[:, None], head_keys[None], head_values[None], owners, places, key_owner, key_place, key_live, scale_factor)
            return (numer / total[..., None])[0]
        outputs = lax.map(per_head, (block_queries, joined_keys, joined_values))
        return outputs.transpose(2, 0, 1, 3).reshape(PAGE_TOKENS, QUERY_HEADS * HEAD_SIZE).astype(jnp.bfloat16)
    attended = lax.map(per_block, (grouped_query_blocks, owner_blocks, place_blocks)).reshape(NEW_TOKEN_COUNT, QUERY_HEADS * HEAD_SIZE)
    return jnp.dot(attended, out_weight, preferred_element_type=jnp.float32).astype(jnp.bfloat16)
```

```python
import functools
import math

import jax
import jax.numpy as jnp
from jax import lax
from jax.experimental import pallas as pl
from jax.experimental.pallas import tpu as pltpu
from jax.sharding import PartitionSpec as P

F32 = jnp.float32
BF16 = jnp.bfloat16
I32 = jnp.int32

MASKED = -1e30
LOWEST = -1e20
LIST = 64
VMEM_BYTES = 32 * 1024 * 1024


def smem():
    return pl.BlockSpec(memory_space=pltpu.SMEM)


def vmem():
    return pl.BlockSpec(memory_space=pltpu.VMEM)


def anywhere():
    return pl.BlockSpec(memory_space=pl.ANY)


def plan_kernel(requests, most, page_size, me_ref, table_ref, len_ref, plan_ref):
    me = me_ref[0]
    counts = 3 * requests * LIST
    for item in range(3 * requests):
        plan_ref[counts + item] = 0
    for r in range(requests):
        length = len_ref[r]

        def page(j, _, r=r, length=length):
            slot = table_ref[r, j]
            relative = (slot // 16) ^ me
            local = slot % 16

            @pl.when(relative < 4)
            def _():
                late = relative >= 2
                high = local >= 8
                phase = jnp.where(late, jnp.where(high, 2, 1), 0)
                place = jnp.where(
                    late,
                    jnp.where(high, (relative - 2) * 8 + local - 8, (relative - 2) * 9 + local),
                    relative * 17 + local,
                )
                live = jnp.minimum(length - j * page_size, page_size)
                which = phase * requests + r
                at = plan_ref[counts + which]
                plan_ref[which * LIST + at] = place * 256 + live
                plan_ref[which * LIST + at + 1] = place * 256
                plan_ref[counts + which] = at + 1

            return 0

        lax.fori_loop(0, (length + page_size - 1) // page_size, page, 0)


def make_plan(me, block_table, cache_len, page_size):
    requests, most = block_table.shape
    return pl.pallas_call(
        functools.partial(plan_kernel, requests, most, page_size),
        out_shape=jax.ShapeDtypeStruct((1024,), I32),
        in_specs=[smem()] * 3,
        out_specs=smem(),
        name="plan",
    )(me, block_table, cache_len)


def attend_kernel(
    phase, pieces, stride, fresh, first, last, scale, requests, width, *refs
):
    refs = list(refs)
    me_ref, plan_ref, start_ref = refs[:3]
    del refs[:3]
    piece_refs = refs[: len(pieces)]
    del refs[: len(pieces)]
    if first:
        query_refs = refs[:4]
        del refs[:4]
        qt_ref, acc_ref, high_ref, sum_ref = refs[:4]
        del refs[:4]
    else:
        qt_ref, acc_in, high_in, sum_in = refs[:4]
        del refs[:4]
        if last:
            message_refs = refs[:4]
            del refs[:4]
            acc_ref, high_ref, sum_ref = refs[:3]
            del refs[:3]
        else:
            acc_ref, high_ref, sum_ref = refs[:3]
            del refs[:3]
    keys_ref, values_ref, sems = refs
    me = me_ref[0]
    columns = qt_ref.shape[2]
    heads = columns // 128
    counts = 3 * requests * LIST

    copies = []
    for n, ((what, source_at, count, slot), ref) in enumerate(zip(pieces, piece_refs)):
        target = keys_ref if what == "k" else values_ref
        source = ref.at[pl.ds(source_at, count)]
        copy = pltpu.make_async_copy(source, target.at[pl.ds(slot, count)], sems.at[n])
        copy.start()
        copies.append(copy)

    if first:
        for k in range(4):
            for h in range(heads):
                block = query_refs[k][:, h * 128 : (h + 1) * 128]
                qt_ref[k, :, h * 128 : (h + 1) * 128] = block.T
            acc_ref[k] = jnp.zeros(acc_ref.shape[1:], F32)
            high_ref[k] = jnp.full(high_ref.shape[1:], LOWEST, F32)
            sum_ref[k] = jnp.zeros(sum_ref.shape[1:], F32)
    else:
        acc_ref[...] = acc_in[...]
        high_ref[...] = high_in[...]
        sum_ref[...] = sum_in[...]
    for copy in copies:
        copy.wait()

    lane = lax.broadcasted_iota(I32, (1, width), 1) % 128

    def absorb(k, at, key_block, value_block, bias):
        cols = pl.ds(at, width)
        scores = jnp.dot(key_block, qt_ref[k, :, cols], preferred_element_type=F32)
        scores = bias(scores * scale)
        before = high_ref[k, :, cols]
        high = jnp.maximum(before, jnp.max(scores, axis=0, keepdims=True))
        weights = jnp.exp2(scores - high)
        shrink = jnp.exp2(before - high)
        high_ref[k, :, cols] = high
        sum_ref[k, :, cols] = sum_ref[k, :, cols] * shrink + jnp.sum(weights, axis=0, keepdims=True)
        part = lax.dot_general(
            value_block,
            weights.astype(BF16),
            (((0,), (0,)), ((), ())),
            preferred_element_type=F32,
        )
        acc_ref[k, :, cols] = acc_ref[k, :, cols] * shrink + part

    def token_block(k, _):
        number = ((me // 4 + 4 - k) % 4) * 4 + me % 4
        low = number * 128

        def request(r, _):
            begin, end = start_ref[r], start_ref[r + 1]
            which = phase * requests + r
            count = plan_ref[counts + which]

            @pl.when((begin < low + 128) & (end > low))
            def _():
                token = lane + low
                column_bias = jnp.where((token >= begin) & (token < end), 0.0, MASKED)

                def pair(i, _):
                    one = plan_ref[which * LIST + 2 * i]
                    two = plan_ref[which * LIST + 2 * i + 1]
                    key_block = jnp.concatenate([keys_ref[one // 256], keys_ref[two // 256]], axis=0)
                    value_block = jnp.concatenate(
                        [values_ref[one // 256], values_ref[two // 256]], axis=0
                    )
                    row = lax.broadcasted_iota(I32, (256, 1), 0)
                    live = jnp.where(row < 128, one % 256, two % 256 + 128)
                    row_bias = jnp.where(row < live, 0.0, MASKED)
                    for at in range(0, columns, width):
                        absorb(
                            k, at, key_block, value_block, lambda s: s + row_bias + column_bias
                        )
                    return 0

                lax.fori_loop(0, (count + 1) // 2, pair, 0)

            return 0

        lax.fori_loop(0, requests, request, 0)

        for slot, relative in fresh:
            other = me ^ relative
            first_begin = jnp.int32(0)
            for r in range(1, requests):
                first_begin = jnp.where(start_ref[r] <= low, start_ref[r], first_begin)

            @pl.when((other <= number) & (other * 128 + 127 >= first_begin))
            def _():
                token = lane + low
                begin = jnp.zeros((1, width), I32)
                for r in range(1, requests):
                    begin = jnp.where(token >= start_ref[r], start_ref[r], begin)
                key_token = lax.broadcasted_iota(I32, (128, 1), 0) + other * 128
                for at in range(0, columns, width):
                    absorb(
                        k,
                        at,
                        keys_ref[slot],
                        values_ref[slot],
                        lambda s: jnp.where(
                            (key_token <= token) & (key_token >= begin), s, MASKED
                        ),
                    )

        return 0

    lax.fori_loop(0, 4, token_block, 0)

    if last:
        for k in range(4):
            total = sum_ref[k]
            some = total > 0.0
            inverse = jnp.where(some, 1.0 / jnp.where(some, total, 1.0), 0.0)
            level = jnp.where(some, high_ref[k] + jnp.log2(jnp.where(some, total, 1.0)), MASKED)
            levels = []
            for h in range(heads):
                cols = slice(h * 128, (h + 1) * 128)
                message_refs[k][h * 128 : (h + 1) * 128, :] = (
                    acc_ref[k, :, cols] * inverse[:, cols]
                ).astype(BF16)
                levels.append(level[:, cols])
            level = jnp.concatenate(levels, axis=0)
            one = level.astype(BF16)
            rest = level - one.astype(F32)
            two = rest.astype(BF16)
            three = (rest - two.astype(F32)).astype(BF16)
            tail = jnp.concatenate(
                [one.astype(F32), two.astype(F32), three.astype(F32), jnp.zeros_like(level)], axis=0
            )
            message_refs[k][heads * 128 :, :] = tail.astype(BF16)


def attend(phase, pieces, arrays, stride, slots, fresh, me, plan, new_start, scale, queries=None, state=None, last=False):
    first = state is None
    requests = new_start.shape[0] - 1
    columns = queries[0].shape[1] if first else state[0].shape[2]
    state_shapes = [
        jax.ShapeDtypeStruct((4, 128, columns), F32),
        jax.ShapeDtypeStruct((4, 1, columns), F32),
        jax.ShapeDtypeStruct((4, 1, columns), F32),
    ]
    scratch = [
        pltpu.VMEM((slots, 128, 128), BF16),
        pltpu.VMEM((slots, 128, 128), BF16),
        pltpu.SemaphoreType.DMA((len(pieces),)),
    ]
    if first:
        more = list(queries)
        out_shape = [jax.ShapeDtypeStruct((4, 128, columns), BF16)] + state_shapes
    else:
        more = list(state)
        if last:
            rows = columns + 4 * (columns // 128)
            out_shape = [jax.ShapeDtypeStruct((rows, 128), BF16)] * 4
            scratch = [pltpu.VMEM(s.shape, s.dtype) for s in state_shapes] + scratch
        else:
            out_shape = state_shapes
    return pl.pallas_call(
        functools.partial(
            attend_kernel, phase, pieces, stride, fresh, first, last, scale, requests, 256
        ),
        out_shape=out_shape,
        in_specs=[smem()] * 3 + [anywhere()] * len(arrays) + [vmem()] * len(more),
        out_specs=[vmem()] * len(out_shape),
        scratch_shapes=scratch,
        compiler_params=pltpu.CompilerParams(vmem_limit_bytes=VMEM_BYTES),
        cost_estimate=pl.CostEstimate(flops=2_000_000_000, bytes_accessed=8_000_000, transcendentals=4_000_000),
        name=f"attend_{phase}",
    )(me, plan, new_start, *arrays, *more)


def merge_kernel(heads, *refs):
    messages, out_ref = refs[:4], refs[4]
    tails = [m[heads * 128 :, :].astype(F32) for m in messages]
    levels = [t[:heads] + t[heads : 2 * heads] + t[2 * heads : 3 * heads] for t in tails]
    top = functools.reduce(jnp.maximum, levels)
    weights = [jnp.exp2(level - top) for level in levels]
    total = functools.reduce(jnp.add, weights)
    weights = [w / total for w in weights]
    for h in range(heads):
        rows = slice(h * 128, (h + 1) * 128)
        value = sum(m[rows, :].astype(F32) * w[h : h + 1, :] for m, w in zip(messages, weights))
        out_ref[:, rows] = value.T.astype(BF16)


def merge(messages, heads):
    return pl.pallas_call(
        functools.partial(merge_kernel, heads),
        out_shape=jax.ShapeDtypeStruct((128, heads * 128), BF16),
        in_specs=[vmem()] * 4,
        out_specs=vmem(),
        compiler_params=pltpu.CompilerParams(vmem_limit_bytes=VMEM_BYTES),
        cost_estimate=pl.CostEstimate(flops=2_000_000, bytes_accessed=1_300_000, transcendentals=4096),
        name="merge",
    )(*messages)


def project_kernel(target_ref, x_ref, w_ref, out_ref):
    out_ref[...] = jnp.dot(x_ref[...], w_ref[...], preferred_element_type=F32).astype(out_ref.dtype)


def project(target, attended, out_weight, wide, dtype):
    rows, depth = attended.shape
    tile = 512
    steps = wide // tile
    return pl.pallas_call(
        project_kernel,
        grid_spec=pltpu.PrefetchScalarGridSpec(
            num_scalar_prefetch=1,
            grid=(steps,),
            in_specs=[
                pl.BlockSpec((rows, depth), lambda i, t: (0, 0)),
                pl.BlockSpec((depth, tile), lambda i, t: (0, t[0] * steps + i)),
            ],
            out_specs=pl.BlockSpec((rows, tile), lambda i, t: (0, i)),
        ),
        out_shape=jax.ShapeDtypeStruct((rows, wide), dtype),
        compiler_params=pltpu.CompilerParams(vmem_limit_bytes=VMEM_BYTES),
        cost_estimate=pl.CostEstimate(
            flops=2 * rows * depth * wide, bytes_accessed=2 * depth * wide, transcendentals=0
        ),
        name="project",
    )(target, attended, out_weight)


def swap(value, axis, mask):
    return lax.ppermute(value, axis, [(i, i ^ mask) for i in range(lax.axis_size(axis))])


def forward(value, axis, by):
    count = lax.axis_size(axis)
    return lax.ppermute(value, axis, [(i, (i + by) % count) for i in range(count)])


def on_device(
    queries,
    incoming_keys,
    incoming_values,
    paged_key_cache,
    paged_value_cache,
    block_table,
    cache_len,
    new_start,
    out_weight,
):
    position = lax.axis_index("ctx")
    column = lax.axis_index("head")
    head_count = lax.axis_size("head")
    page_size, head_width = paged_key_cache.shape[2:]
    heads = queries.shape[1] // head_width
    scale = math.log2(math.e) / math.sqrt(head_width)
    me = position.astype(I32).reshape(1)

    keys = paged_key_cache.reshape(-1, page_size, head_width)
    values = paged_value_cache.reshape(-1, page_size, head_width)
    new_keys = incoming_keys.reshape(1, page_size, head_width)
    new_values = incoming_values.reshape(1, page_size, head_width)
    half_a = jnp.concatenate([keys[:8], new_keys, values[:8], new_values], axis=0)
    half_b = jnp.concatenate([keys[8:], values[8:]], axis=0)

    far_a = swap(half_a, "ctx", 2)
    far_b = swap(half_b, "ctx", 2)
    near_a = swap(half_a, "ctx", 1)
    near_b = swap(half_b, "ctx", 1)
    all_queries = [queries] + [forward(queries, "ctx", 4 * k) for k in range(1, 4)]
    plan = make_plan(me, block_table, cache_len, page_size)

    pieces = (
        ("k", 0, 16, 0), ("k", 0, 1, 16), ("v", 0, 16, 0), ("v", 0, 1, 16),
        ("k", 0, 8, 17), ("k", 8, 1, 33), ("v", 9, 8, 17), ("v", 17, 1, 33),
        ("k", 0, 8, 25), ("v", 8, 8, 25),
    )
    arrays = [keys, new_keys, values, new_values, near_a, near_a, near_a, near_a, near_b, near_b]
    state = attend(
        0, pieces, arrays, 17, 34, ((16, 0), (33, 1)), me, plan, new_start, scale, queries=all_queries
    )
    far_near_a = swap(far_a, "ctx", 1)
    pieces = (("k", 0, 9, 0), ("v", 9, 9, 0), ("k", 0, 9, 9), ("v", 9, 9, 9))
    state = [state[0]] + list(
        attend(
            1, pieces, [far_a, far_a, far_near_a, far_near_a], 9, 18, ((8, 2), (17, 3)),
            me, plan, new_start, scale, state=state,
        )
    )
    far_near_b = swap(far_b, "ctx", 1)
    pieces = (("k", 0, 8, 0), ("v", 8, 8, 0), ("k", 0, 8, 8), ("v", 8, 8, 8))
    messages = attend(
        2, pieces, [far_b, far_b, far_near_b, far_near_b], 8, 16, (),
        me, plan, new_start, scale, state=state, last=True,
    )
    received = [messages[0]] + [forward(messages[k], "ctx", -4 * k) for k in range(1, 4)]
    attended = merge(received, heads)

    wide = out_weight.shape[1] // head_count
    shares = []
    for mask in (5, 4, 3, 7, 2, 6, 1):
        target = (column ^ mask).astype(I32).reshape(1)
        shares.append(swap(project(target, attended, out_weight, wide, BF16), "head", mask))
    total = project(column.astype(I32).reshape(1), attended, out_weight, wide, F32)
    for share in shares:
        total = total + share.astype(F32)
    return total.astype(BF16)


def solution(mesh):
    return jax.shard_map(
        on_device,
        mesh=mesh,
        in_specs=(
            P("ctx", "head"),
            P("ctx", "head"),
            P("ctx", "head"),
            P("ctx", "head", None, None),
            P("ctx", "head", None, None),
            P(),
            P(),
            P(),
            P("head", None),
        ),
        out_specs=P("ctx", "head"),
        check_vma=False,
    )
```

```python
import functools
import math

import jax
import jax.numpy as jnp
from jax import lax
from jax.experimental import pallas as pl
from jax.experimental.pallas import tpu as pltpu
from jax.sharding import PartitionSpec as P

F32 = jnp.float32
BF16 = jnp.bfloat16
I32 = jnp.int32

MASKED = -1e30
LOWEST = -1e20
LIST = 64
TASKS = 128
FIELDS = 8
FAR = 1 << 20
VMEM_BYTES = 24 * 1024 * 1024
SMALL_VMEM_BYTES = 8 * 1024 * 1024


def smem():
    return pl.BlockSpec(memory_space=pltpu.SMEM)


def vmem():
    return pl.BlockSpec(memory_space=pltpu.VMEM)


def anywhere():
    return pl.BlockSpec(memory_space=pl.ANY)


def plan_kernel(requests, blocks, page_size, me_ref, table_ref, len_ref, start_ref, *refs):
    outs, slot_ref, code_ref, count_ref = refs[:2], refs[2], refs[3], refs[4]
    me = me_ref[0]
    spare = 2 * requests * LIST

    for r in range(requests):
        length = len_ref[r]

        def pages(i, counts, r=r, length=length):
            near, far = counts
            for u in range(4):
                j = 4 * i + u
                slot = table_ref[r, j]
                relative = (slot >> 4) ^ me
                live = length - j * page_size
                mine = (relative < 4) & (live > 0)
                is_far = relative >= 2
                at = jnp.where(is_far, (requests + r) * LIST + far, r * LIST + near)
                at = jnp.where(mine, at, spare)
                slot_ref[at] = (relative & 1) * (blocks + 1) + (slot & 15)
                code_ref[at] = jnp.minimum(live, page_size)
                one = jnp.where(mine, 1, 0)
                far_one = jnp.where(is_far, one, 0)
                near, far = near + one - far_one, far + far_one
            return near, far

        near, far = lax.fori_loop(
            0, (length + 4 * page_size - 1) // (4 * page_size), pages, (jnp.int32(0), jnp.int32(0))
        )
        count_ref[r] = near
        count_ref[requests + r] = far

    for phase in range(2):
        out = outs[phase]

        def step(item, first, phase=phase, out=out):
            k, r = item // requests, item % requests
            number = ((me // 4 + 4 - k) % 4) * 4 + me % 4
            low = number * 128
            begin, end = start_ref[r], start_ref[r + 1]
            which = phase * requests + r
            base = which * LIST
            total = count_ref[which]
            for side in range(2):
                other = me ^ (2 * phase + side)
                slot_ref[base + total] = side * (blocks + 1) + blocks
                code_ref[base + total] = -1 - other
                meets = (other <= number) & (begin < other * 128 + 128) & (end > other * 128)
                total = total + jnp.where(meets, 1, 0)
            slot_ref[base + total] = 0
            code_ref[base + total] = 0
            whole = (begin <= low) & (end >= low + 128)
            pairs = jnp.where((begin < low + 128) & (end > low), (total + 1) // 2, 0)

            def task(i, _):
                at = (first + i) * FIELDS
                one, two = code_ref[base + 2 * i], code_ref[base + 2 * i + 1]
                out[at] = k
                out[at + 1] = slot_ref[base + 2 * i]
                out[at + 2] = slot_ref[base + 2 * i + 1]
                out[at + 3] = one
                out[at + 4] = two
                out[at + 5] = jnp.where(whole & (one == page_size) & (two == page_size), 0, 1)
                out[at + 6] = low
                out[at + 7] = r
                return 0

            lax.fori_loop(0, pairs, task, 0)
            return first + pairs

        last = lax.fori_loop(0, 4 * requests, step, jnp.int32(0))
        out[TASKS * FIELDS] = last
        for extra in range(2):
            for field in range(FIELDS):
                out[(last + extra) * FIELDS + field] = 1 if field == 5 else 0


def make_plan(me, block_table, cache_len, new_start, blocks, page_size):
    requests = block_table.shape[0]
    return pl.pallas_call(
        functools.partial(plan_kernel, requests, blocks, page_size),
        out_shape=[jax.ShapeDtypeStruct((TASKS * FIELDS + 128,), I32)] * 2,
        in_specs=[smem()] * 4,
        out_specs=[smem()] * 2,
        scratch_shapes=[
            pltpu.SMEM((2 * requests * LIST + 8,), I32),
            pltpu.SMEM((2 * requests * LIST + 8,), I32),
            pltpu.SMEM((2 * requests,), I32),
        ],
        cost_estimate=pl.CostEstimate(flops=4_000_000_000, bytes_accessed=8_000_000, transcendentals=0),
        name="plan",
    )(me, block_table, cache_len, new_start)


def run_tasks(plan_ref, start_ref, qt_ref, keys_ref, values_ref, scores_ref, acc_ref, high_ref, sum_ref, scale, width):
    columns = qt_ref.shape[2]
    starts = list(range(0, columns, width))

    def score(task, place):
        at = task * FIELDS
        k = plan_ref[at]
        key_block = jnp.concatenate([keys_ref[plan_ref[at + 1]], keys_ref[plan_ref[at + 2]]], axis=0)
        for c in starts:
            scores_ref[place, :, c : c + width] = jnp.dot(
                key_block, qt_ref[k, :, c : c + width], preferred_element_type=F32
            )

    def absorb(task, place, masked):
        at = task * FIELDS
        k = plan_ref[at]
        value_block = jnp.concatenate(
            [values_ref[plan_ref[at + 1]].T, values_ref[plan_ref[at + 2]].T], axis=1
        )
        value_block = jnp.concatenate([value_block, jnp.ones((16, 256), BF16)], axis=0)
        if masked:
            low, r = plan_ref[at + 6], plan_ref[at + 7]
            begin, end = start_ref[r], start_ref[r + 1]
            row = lax.broadcasted_iota(I32, (128, 1), 0)
            rows = []
            for field in (3, 4):
                code = plan_ref[at + field]
                token = row - (code + 1) * 128
                rows.append(
                    jnp.where(
                        code >= 0,
                        jnp.where(row < code, -1, FAR),
                        jnp.where((token >= begin) & (token < end), token, FAR),
                    )
                )
            key_token = jnp.concatenate(rows, axis=0)
            token = low + lax.broadcasted_iota(I32, (1, width), 1) % 128
            query_token = jnp.where((token >= begin) & (token < end), token, -2)
        for c in starts:
            cols = slice(c, c + width)
            scores = scores_ref[place, :, cols]
            if masked:
                scores = jnp.where(key_token <= query_token, scores, MASKED)
            before = high_ref[k, :, cols]
            high = jnp.maximum(before, jnp.max(scores, axis=0, keepdims=True))
            weights = jnp.exp2(scores * scale - high * scale)
            shrink = jnp.exp2((before - high) * scale)
            part = jnp.dot(value_block, weights.astype(BF16), preferred_element_type=F32)
            high_ref[k, :, cols] = high
            sum_ref[k, :, cols] = sum_ref[k, :, cols] * shrink + part[128:129]
            acc_ref[k, :, cols] = acc_ref[k, :, cols] * shrink + part[:128]

    def step(task, place):
        masked = plan_ref[task * FIELDS + 5]

        @pl.when(masked == 0)
        def _():
            score(task + 1, 1 - place)
            absorb(task, place, False)

        @pl.when(masked != 0)
        def _():
            score(task + 1, 1 - place)
            absorb(task, place, True)

    def two(i, _):
        step(2 * i, 0)
        step(2 * i + 1, 1)
        return 0

    score(0, 0)
    lax.fori_loop(0, (plan_ref[TASKS * FIELDS] + 1) // 2, two, 0)


def clear(acc_ref, high_ref, sum_ref):
    acc_ref[...] = jnp.zeros(acc_ref.shape, F32)
    high_ref[...] = jnp.full(high_ref.shape, LOWEST, F32)
    sum_ref[...] = jnp.zeros(sum_ref.shape, F32)


def near_kernel(scale, width, plan_ref, start_ref, own_ref, near_ref, q0, q1, q2, q3, *refs):
    qt_ref, acc_ref, high_ref, sum_ref, q_ref, keys_ref, values_ref, scores_ref, sems = refs
    columns = qt_ref.shape[2]
    blocks = own_ref.shape[0] // 2
    queries = [
        pltpu.make_async_copy(ref, q_ref.at[k], sems.at[k]) for k, ref in enumerate((q0, q1, q2, q3))
    ]
    copies = []
    for side, ref in enumerate((own_ref, near_ref)):
        to = pl.ds(side * blocks, blocks)
        copies.append(pltpu.make_async_copy(ref.at[pl.ds(0, blocks)], keys_ref.at[to], sems.at[4 + side]))
        copies.append(pltpu.make_async_copy(ref.at[pl.ds(blocks, blocks)], values_ref.at[to], sems.at[6 + side]))
    for copy in queries + copies:
        copy.start()
    clear(acc_ref, high_ref, sum_ref)
    for k in range(4):
        queries[k].wait()
        for c in range(0, columns, 128):
            qt_ref[k, :, c : c + 128] = q_ref[k, :, c : c + 128].T
    for copy in copies:
        copy.wait()
    run_tasks(plan_ref, start_ref, qt_ref, keys_ref, values_ref, scores_ref, acc_ref, high_ref, sum_ref, scale, width)


def far_kernel(scale, width, plan_ref, start_ref, far_ref, near_ref, qt_in, acc_in, high_in, sum_in, *refs):
    message_refs = refs[:4]
    qt_ref, acc_ref, high_ref, sum_ref, acc_a, high_a, sum_a, keys_ref, values_ref, scores_ref, sems = refs[4:]
    columns = qt_ref.shape[2]
    heads = columns // 128
    blocks = far_ref.shape[0] // 2
    copies = [pltpu.make_async_copy(qt_in, qt_ref, sems.at[0])]
    for side, ref in enumerate((far_ref, near_ref)):
        to = pl.ds(side * blocks, blocks)
        copies.append(pltpu.make_async_copy(ref.at[pl.ds(0, blocks)], keys_ref.at[to], sems.at[1 + side]))
        copies.append(pltpu.make_async_copy(ref.at[pl.ds(blocks, blocks)], values_ref.at[to], sems.at[3 + side]))
    earlier = [
        pltpu.make_async_copy(acc_in, acc_a, sems.at[5]),
        pltpu.make_async_copy(high_in, high_a, sems.at[6]),
        pltpu.make_async_copy(sum_in, sum_a, sems.at[7]),
    ]
    for copy in copies + earlier:
        copy.start()
    clear(acc_ref, high_ref, sum_ref)
    for copy in copies:
        copy.wait()
    run_tasks(plan_ref, start_ref, qt_ref, keys_ref, values_ref, scores_ref, acc_ref, high_ref, sum_ref, scale, width)
    for copy in earlier:
        copy.wait()

    for k in range(4):
        high = jnp.maximum(high_ref[k], high_a[k])
        shrink_a = jnp.exp2((high_a[k] - high) * scale)
        shrink = jnp.exp2((high_ref[k] - high) * scale)
        total = sum_a[k] * shrink_a + sum_ref[k] * shrink
        some = total > 0.0
        safe = jnp.where(some, total, 1.0)
        inverse = jnp.where(some, 1.0 / safe, 0.0)
        level = jnp.where(some, high * scale + jnp.log2(safe), MASKED)
        factor_a, factor = shrink_a * inverse, shrink * inverse
        levels = []
        for h in range(heads):
            cols = slice(h * 128, (h + 1) * 128)
            message_refs[k][cols, :] = (
                acc_a[k, :, cols] * factor_a[:, cols] + acc_ref[k, :, cols] * factor[:, cols]
            ).astype(BF16)
            levels.append(level[:, cols])
        level = jnp.concatenate(levels, axis=0)
        one = level.astype(BF16)
        rest = level - one.astype(F32)
        two = rest.astype(BF16)
        three = (rest - two.astype(F32)).astype(BF16)
        tail = jnp.concatenate(
            [one.astype(F32), two.astype(F32), three.astype(F32), jnp.zeros_like(level)], axis=0
        )
        message_refs[k][heads * 128 :, :] = tail.astype(BF16)


def state_shapes(columns):
    return [(4, 128, columns), (4, 1, columns), (4, 1, columns)]


def key_scratch(blocks, columns):
    return [
        pltpu.VMEM((2 * blocks, 128, 128), BF16),
        pltpu.VMEM((2 * blocks, 128, 128), BF16),
        pltpu.VMEM((2, 256, columns), F32),
        pltpu.SemaphoreType.DMA((8,)),
    ]


def attend_near(plan, new_start, own, near, queries, scale):
    rows, columns = queries[0].shape
    return pl.pallas_call(
        functools.partial(near_kernel, scale, 256),
        out_shape=[jax.ShapeDtypeStruct((4, 128, columns), BF16)]
        + [jax.ShapeDtypeStruct(s, F32) for s in state_shapes(columns)],
        in_specs=[smem()] * 2 + [anywhere()] * 6,
        out_specs=[vmem()] * 4,
        scratch_shapes=[pltpu.VMEM((4, rows, columns), BF16)] + key_scratch(own.shape[0] // 2, columns),
        compiler_params=pltpu.CompilerParams(vmem_limit_bytes=VMEM_BYTES),
        cost_estimate=pl.CostEstimate(flops=8_000_000_000, bytes_accessed=8_000_000, transcendentals=4_000_000),
        name="attend_near",
    )(plan, new_start, own, near, *queries)


def attend_far(plan, new_start, far, far_near, state, scale):
    columns = state[0].shape[2]
    rows = columns + 4 * (columns // 128)
    states = [pltpu.VMEM(s, F32) for s in state_shapes(columns)]
    return pl.pallas_call(
        functools.partial(far_kernel, scale, 256),
        out_shape=[jax.ShapeDtypeStruct((rows, 128), BF16)] * 4,
        in_specs=[smem()] * 2 + [anywhere()] * 6,
        out_specs=[vmem()] * 4,
        scratch_shapes=[pltpu.VMEM((4, 128, columns), BF16)]
        + states
        + states
        + key_scratch(far.shape[0] // 2, columns),
        compiler_params=pltpu.CompilerParams(vmem_limit_bytes=VMEM_BYTES),
        cost_estimate=pl.CostEstimate(flops=8_000_000_000, bytes_accessed=8_000_000, transcendentals=4_000_000),
        name="attend_far",
    )(plan, new_start, far, far_near, *state)


def merged(messages, heads, out_ref):
    tails = [m[heads * 128 :, :].astype(F32) for m in messages]
    levels = [t[:heads] + t[heads : 2 * heads] + t[2 * heads : 3 * heads] for t in tails]
    top = functools.reduce(jnp.maximum, levels)
    weights = [jnp.exp2(level - top) for level in levels]
    total = functools.reduce(jnp.add, weights)
    weights = [w / total for w in weights]
    for h in range(heads):
        rows = slice(h * 128, (h + 1) * 128)
        value = sum(m[rows, :].astype(F32) * w[h : h + 1, :] for m, w in zip(messages, weights))
        out_ref[:, rows] = value.T.astype(BF16)


def merge_kernel(heads, *refs):
    merged(refs[:4], heads, refs[4])


def merge(messages, heads):
    return pl.pallas_call(
        functools.partial(merge_kernel, heads),
        out_shape=jax.ShapeDtypeStruct((128, heads * 128), BF16),
        in_specs=[vmem()] * 4,
        out_specs=vmem(),
        compiler_params=pltpu.CompilerParams(vmem_limit_bytes=SMALL_VMEM_BYTES),
        cost_estimate=pl.CostEstimate(flops=2_000_000, bytes_accessed=1_300_000, transcendentals=4096),
        name="merge",
    )(*messages)


def bring_kernel(wide, targets_ref, source_ref, *refs):
    outs, sems = refs[:-1], refs[-1]
    pieces = 2
    step = source_ref.shape[0] // pieces
    copies = []
    for n, out in enumerate(outs):
        at = pl.multiple_of(targets_ref[n] * wide, wide)
        for p in range(pieces):
            rows = pl.ds(p * step, step)
            copies.append(
                pltpu.make_async_copy(
                    source_ref.at[rows, pl.ds(at, wide)], out.at[rows], sems.at[n * pieces + p]
                )
            )
            copies[-1].start()
    for copy in copies:
        copy.wait()


def bring(targets, value, wide):
    count = targets.shape[0]
    depth = value.shape[0]
    return pl.pallas_call(
        functools.partial(bring_kernel, wide),
        out_shape=[jax.ShapeDtypeStruct((depth, wide), value.dtype)] * count,
        in_specs=[smem(), anywhere()],
        out_specs=[vmem()] * count,
        scratch_shapes=[pltpu.SemaphoreType.DMA((2 * count,))],
        compiler_params=pltpu.CompilerParams(vmem_limit_bytes=VMEM_BYTES),
        cost_estimate=pl.CostEstimate(flops=0, bytes_accessed=2 * value.size * 2, transcendentals=0),
        name="bring",
    )(targets, value)


def project_kernel(x_ref, w_ref, out_ref):
    out_ref[...] = jnp.dot(x_ref[...], w_ref[...], preferred_element_type=F32).astype(out_ref.dtype)


def project(attended, weight, dtype):
    rows, depth = attended.shape
    wide = weight.shape[1]
    return pl.pallas_call(
        project_kernel,
        out_shape=jax.ShapeDtypeStruct((rows, wide), dtype),
        in_specs=[vmem()] * 2,
        out_specs=vmem(),
        compiler_params=pltpu.CompilerParams(vmem_limit_bytes=SMALL_VMEM_BYTES),
        cost_estimate=pl.CostEstimate(
            flops=2 * rows * depth * wide, bytes_accessed=2 * depth * wide, transcendentals=0
        ),
        name="project",
    )(attended, weight)


def swap(value, axis, mask):
    return lax.ppermute(value, axis, [(i, i ^ mask) for i in range(lax.axis_size(axis))])


def forward(value, axis, by):
    count = lax.axis_size(axis)
    return lax.ppermute(value, axis, [(i, (i + by) % count) for i in range(count)])


def on_device(
    queries,
    incoming_keys,
    incoming_values,
    paged_key_cache,
    paged_value_cache,
    block_table,
    cache_len,
    new_start,
    out_weight,
):
    position = lax.axis_index("ctx")
    column = lax.axis_index("head")
    head_count = lax.axis_size("head")
    blocks = paged_key_cache.shape[0]
    page_size, head_width = paged_key_cache.shape[2:]
    scale = math.log2(math.e) / math.sqrt(head_width)
    wide = out_weight.shape[1] // head_count
    masks = (5, 4, 3, 7, 2, 6, 1)
    me = position.astype(I32).reshape(1)

    def as_blocks(value):
        return value.reshape(-1, page_size, head_width)

    own = jnp.concatenate(
        [as_blocks(v) for v in (paged_key_cache, incoming_keys, paged_value_cache, incoming_values)], axis=0
    )
    far = swap(own, "ctx", 2)
    near = swap(own, "ctx", 1)
    query_one = forward(queries, "ctx", 4)
    query_three = forward(queries, "ctx", 12)
    plan = make_plan(me, block_table, cache_len, new_start, blocks, page_size)
    query_two = forward(queries, "ctx", 8)
    state = attend_near(
        plan[0], new_start, own, near, [queries, query_one, query_two, query_three], scale
    )
    far, state = lax.optimization_barrier((far, state))
    far_near = swap(far, "ctx", 1)
    messages = attend_far(plan[1], new_start, far, far_near, state, scale)
    out_weight, *messages = lax.optimization_barrier([out_weight, *messages])
    weights = bring(column ^ jnp.array(masks + (0,), I32), out_weight, wide)
    received = [messages[0]] + [forward(messages[k], "ctx", -4 * k) for k in range(1, 4)]

    attended = merge(received, queries.shape[1] // head_width)
    shares = [
        swap(project(attended, weight, BF16), "head", mask) for mask, weight in zip(masks, weights)
    ]
    total = project(attended, weights[-1], F32)
    for share in shares:
        total = total + share.astype(F32)
    return total.astype(BF16)


def solution(mesh):
    return jax.shard_map(
        on_device,
        mesh=mesh,
        in_specs=(
            P("ctx", "head"),
            P("ctx", "head"),
            P("ctx", "head"),
            P("ctx", "head", None, None),
            P("ctx", "head", None, None),
            P(),
            P(),
            P(),
            P("head", None),
        ),
        out_specs=P("ctx", "head"),
        check_vma=False,
    )
```

```python
import functools
import math

import jax
import jax.numpy as jnp
from jax import lax
from jax.experimental import pallas as pl
from jax.experimental.pallas import tpu as pltpu
from jax.sharding import PartitionSpec as P

F32 = jnp.float32
BF16 = jnp.bfloat16
I32 = jnp.int32

MASKED = -1e30
LOWEST = -1e20
LIST = 64
TASKS = 128
FIELDS = 8
FAR = 1 << 20
VMEM_BYTES = 14 * 1024 * 1024
LARGE_VMEM_BYTES = 30 * 1024 * 1024
SMALL_VMEM_BYTES = 8 * 1024 * 1024


def smem():
    return pl.BlockSpec(memory_space=pltpu.SMEM)


def vmem():
    return pl.BlockSpec(memory_space=pltpu.VMEM)


def anywhere():
    return pl.BlockSpec(memory_space=pl.ANY)


def hbm():
    return pl.BlockSpec(memory_space=pltpu.HBM)


def plan_kernel(requests, blocks, page_size, me_ref, table_ref, len_ref, start_ref, *refs):
    outs, slot_ref, code_ref, count_ref = refs[:4], refs[4], refs[5], refs[6]
    me = me_ref[0]
    spare = 2 * requests * LIST

    for r in range(requests):
        length = len_ref[r]

        def pages(i, counts, r=r, length=length):
            near, far = counts
            for u in range(4):
                j = 4 * i + u
                slot = table_ref[r, j]
                relative = (slot >> 4) ^ me
                live = length - j * page_size
                mine = (relative < 4) & (live > 0)
                is_far = relative >= 2
                at = jnp.where(is_far, (requests + r) * LIST + far, r * LIST + near)
                at = jnp.where(mine, at, spare)
                slot_ref[at] = (relative & 1) * (blocks + 1) + (slot & 15)
                code_ref[at] = jnp.minimum(live, page_size)
                one = jnp.where(mine, 1, 0)
                far_one = jnp.where(is_far, one, 0)
                near, far = near + one - far_one, far + far_one
            return near, far

        near, far = lax.fori_loop(
            0, (length + 4 * page_size - 1) // (4 * page_size), pages, (jnp.int32(0), jnp.int32(0))
        )
        count_ref[r] = near
        count_ref[requests + r] = far

    for out, phase, first_k, last_k in zip(outs, (0, 0, 1, 1), (0, 1, 0, 1), (1, 4, 1, 4)):

        def step(item, first, out=out, phase=phase, first_k=first_k):
            k, r = item // requests + first_k, item % requests
            number = ((me // 4 + 4 - k) % 4) * 4 + me % 4
            low = number * 128
            begin, end = start_ref[r], start_ref[r + 1]
            which = phase * requests + r
            base = which * LIST
            total = count_ref[which]
            for side in range(2):
                other = me ^ (2 * phase + side)
                slot_ref[base + total] = side * (blocks + 1) + blocks
                code_ref[base + total] = -1 - other
                meets = (other <= number) & (begin < other * 128 + 128) & (end > other * 128)
                total = total + jnp.where(meets, 1, 0)
            slot_ref[base + total] = 0
            code_ref[base + total] = 0
            whole = (begin <= low) & (end >= low + 128)
            pairs = jnp.where((begin < low + 128) & (end > low), (total + 1) // 2, 0)

            def task(i, _):
                at = (first + i) * FIELDS
                one, two = code_ref[base + 2 * i], code_ref[base + 2 * i + 1]
                out[at] = k - first_k
                out[at + 1] = slot_ref[base + 2 * i]
                out[at + 2] = slot_ref[base + 2 * i + 1]
                out[at + 3] = one
                out[at + 4] = two
                out[at + 5] = jnp.where(whole & (one == page_size) & (two == page_size), 0, 1)
                out[at + 6] = low
                out[at + 7] = r
                return 0

            lax.fori_loop(0, pairs, task, 0)
            return first + pairs

        last = lax.fori_loop(0, (last_k - first_k) * requests, step, jnp.int32(0))
        out[TASKS * FIELDS] = last
        for extra in range(2):
            for field in range(FIELDS):
                out[(last + extra) * FIELDS + field] = 1 if field == 5 else 0


def make_plan(me, block_table, cache_len, new_start, blocks, page_size):
    requests = block_table.shape[0]
    return pl.pallas_call(
        functools.partial(plan_kernel, requests, blocks, page_size),
        out_shape=[jax.ShapeDtypeStruct((TASKS * FIELDS + 128,), I32)] * 4,
        in_specs=[smem()] * 4,
        out_specs=[smem()] * 4,
        scratch_shapes=[
            pltpu.SMEM((2 * requests * LIST + 8,), I32),
            pltpu.SMEM((2 * requests * LIST + 8,), I32),
            pltpu.SMEM((2 * requests,), I32),
        ],
        cost_estimate=pl.CostEstimate(flops=1_000_000_000, bytes_accessed=100_000, transcendentals=0),
        name="plan",
    )(me, block_table, cache_len, new_start)


def run_tasks(plan_ref, start_ref, qt_ref, keys_ref, values_ref, scores_ref, acc_ref, high_ref, sum_ref, scale, width):
    columns = qt_ref.shape[2]
    starts = list(range(0, columns, width))

    def score(task, place):
        at = task * FIELDS
        k = plan_ref[at]
        key_block = jnp.concatenate([keys_ref[plan_ref[at + 1]], keys_ref[plan_ref[at + 2]]], axis=0)
        for c in starts:
            scores_ref[place, :, c : c + width] = jnp.dot(
                key_block, qt_ref[k, :, c : c + width], preferred_element_type=F32
            )

    def absorb(task, place, masked):
        at = task * FIELDS
        k = plan_ref[at]
        value_block = jnp.concatenate(
            [values_ref[plan_ref[at + 1]].T, values_ref[plan_ref[at + 2]].T], axis=1
        )
        value_block = jnp.concatenate([value_block, jnp.ones((16, 256), BF16)], axis=0)
        if masked:
            low, r = plan_ref[at + 6], plan_ref[at + 7]
            begin, end = start_ref[r], start_ref[r + 1]
            row = lax.broadcasted_iota(I32, (128, 1), 0)
            rows = []
            for field in (3, 4):
                code = plan_ref[at + field]
                token = row - (code + 1) * 128
                rows.append(
                    jnp.where(
                        code >= 0,
                        jnp.where(row < code, -1, FAR),
                        jnp.where((token >= begin) & (token < end), token, FAR),
                    )
                )
            key_token = jnp.concatenate(rows, axis=0)
            token = low + lax.broadcasted_iota(I32, (1, width), 1) % 128
            query_token = jnp.where((token >= begin) & (token < end), token, -2)
        for c in starts:
            cols = slice(c, c + width)
            scores = scores_ref[place, :, cols]
            if masked:
                scores = jnp.where(key_token <= query_token, scores, MASKED)
            before = high_ref[k, :, cols]
            high = jnp.maximum(before, jnp.max(scores, axis=0, keepdims=True))
            weights = jnp.exp2(scores * scale - high * scale)
            shrink = jnp.exp2((before - high) * scale)
            part = jnp.dot(value_block, weights.astype(BF16), preferred_element_type=F32)
            high_ref[k, :, cols] = high
            sum_ref[k, :, cols] = sum_ref[k, :, cols] * shrink + part[128:129]
            acc_ref[k, :, cols] = acc_ref[k, :, cols] * shrink + part[:128]

    def step(task, place):
        masked = plan_ref[task * FIELDS + 5]

        @pl.when(masked == 0)
        def _():
            score(task + 1, 1 - place)
            absorb(task, place, False)

        @pl.when(masked != 0)
        def _():
            score(task + 1, 1 - place)
            absorb(task, place, True)

    def two(i, _):
        step(2 * i, 0)
        step(2 * i + 1, 1)
        return 0

    score(0, 0)
    lax.fori_loop(0, (plan_ref[TASKS * FIELDS] + 1) // 2, two, 0)


def clear(acc_ref, high_ref, sum_ref):
    acc_ref[...] = jnp.zeros(acc_ref.shape, F32)
    high_ref[...] = jnp.full(high_ref.shape, LOWEST, F32)
    sum_ref[...] = jnp.zeros(sum_ref.shape, F32)


def bring(targets_ref, source_ref, outs, sems, wide):
    pieces = 2
    step = source_ref.shape[0] // pieces
    copies = []
    for n, out in enumerate(outs):
        at = pl.multiple_of(targets_ref[n] * wide, wide)
        for p in range(pieces):
            rows = pl.ds(p * step, step)
            copies.append(
                pltpu.make_async_copy(
                    source_ref.at[rows, pl.ds(at, wide)], out.at[rows], sems.at[n * pieces + p]
                )
            )
            copies[-1].start()
    return copies


def attend_kernel(form, *refs):
    refs = list(refs)

    def take(n):
        taken = refs[:n]
        del refs[:n]
        return taken

    count, blocks, scale = form["count"], form["blocks"], form["scale"]
    first, last, wide, weights = form["first"], form["last"], form["wide"], form["weights"]
    plan_ref, start_ref = take(2)
    sets = take(form["sets"])
    if first:
        query_refs = take(count)
    else:
        qt_in, *state_in = take(4)
    if weights:
        targets_ref, weight_ref = take(2)
    if last:
        message_refs = take(count)
    else:
        qt_out, *state_out = take(4)
    block_refs = take(weights)
    qt_ref, keys_ref, values_ref, scores_ref = take(4)
    state = take(3)
    if first:
        q_ref = take(1)[0]
    else:
        earlier = take(3)
    key_sems, query_sems, state_sems, weight_sems = take(4)
    acc_ref, high_ref, sum_ref = state
    columns = qt_ref.shape[2]
    heads = columns // 128

    queries = []
    if first:
        for k, ref in enumerate(query_refs):
            queries.append(pltpu.make_async_copy(ref, q_ref.at[k], query_sems.at[k]))
    else:
        queries.append(pltpu.make_async_copy(qt_in, qt_ref, query_sems.at[0]))
    key_copies, value_copies, state_copies = [], [], []
    for n, ref in enumerate(sets):
        to = pl.ds(n * blocks, blocks)
        key_copies.append(
            pltpu.make_async_copy(ref.at[pl.ds(0, blocks)], keys_ref.at[to], key_sems.at[2 * n])
        )
        value_copies.append(
            pltpu.make_async_copy(ref.at[pl.ds(blocks, blocks)], values_ref.at[to], key_sems.at[2 * n + 1])
        )
    if not first:
        for n, (source, target) in enumerate(zip(state_in, earlier)):
            state_copies.append(pltpu.make_async_copy(source, target, state_sems.at[n]))
    for copy in queries + key_copies + value_copies + state_copies:
        copy.start()
    brought = bring(targets_ref, weight_ref, block_refs, weight_sems, wide) if weights else []
    clear(acc_ref, high_ref, sum_ref)
    for k, copy in enumerate(queries):
        copy.wait()
        if first:
            for c in range(0, columns, 128):
                qt_ref[k, :, c : c + 128] = q_ref[k, :, c : c + 128].T
    outgoing = []
    if not last:
        outgoing.append(pltpu.make_async_copy(qt_ref, qt_out, query_sems.at[count]))
        outgoing[0].start()
    for copy in key_copies + value_copies:
        copy.wait()

    run_tasks(
        plan_ref, start_ref, qt_ref, keys_ref, values_ref, scores_ref, acc_ref, high_ref, sum_ref, scale, 256
    )

    for copy in state_copies:
        copy.wait()
    if not last:
        for n, (source, target) in enumerate(zip(state, state_out)):
            outgoing.append(pltpu.make_async_copy(source, target, state_sems.at[n]))
            outgoing[-1].start()
        for copy in outgoing:
            copy.wait()
        return

    for k in range(count):
        if first:
            high = high_ref[k]
            total = sum_ref[k]
        else:
            acc_a, high_a, sum_a = earlier
            high = jnp.maximum(high_ref[k], high_a[k])
            shrink_a = jnp.exp2((high_a[k] - high) * scale)
            shrink = jnp.exp2((high_ref[k] - high) * scale)
            total = sum_a[k] * shrink_a + sum_ref[k] * shrink
        some = total > 0.0
        safe = jnp.where(some, total, 1.0)
        inverse = jnp.where(some, 1.0 / safe, 0.0)
        level = jnp.where(some, high * scale + jnp.log2(safe), MASKED)
        if not first:
            factor_a, factor = shrink_a * inverse, shrink * inverse
        levels = []
        for h in range(heads):
            cols = slice(h * 128, (h + 1) * 128)
            if first:
                value = acc_ref[k, :, cols] * inverse[:, cols]
            else:
                value = acc_a[k, :, cols] * factor_a[:, cols] + acc_ref[k, :, cols] * factor[:, cols]
            message_refs[k][cols, :] = value.astype(BF16)
            levels.append(level[:, cols])
        level = jnp.concatenate(levels, axis=0)
        one = level.astype(BF16)
        rest = level - one.astype(F32)
        two = rest.astype(BF16)
        three = (rest - two.astype(F32)).astype(BF16)
        tail = jnp.concatenate(
            [one.astype(F32), two.astype(F32), three.astype(F32), jnp.zeros_like(level)], axis=0
        )
        message_refs[k][heads * 128 :, :] = tail.astype(BF16)
    for copy in brought:
        copy.wait()


def attend(plan, new_start, sets, scale, queries=None, state=None, last=False, targets=None, weight=None, wide=0, name="attend"):
    first = state is None
    if first:
        count, columns = len(queries), queries[0].shape[1]
    else:
        count, _, columns = state[0].shape
    blocks = sets[0].shape[0] // 2
    weights = 0 if targets is None else targets.shape[0]
    state_shapes = [(count, 128, columns), (count, 1, columns), (count, 1, columns)]
    rows = columns + 4 * (columns // 128)
    form = dict(
        count=count, blocks=blocks, scale=scale, sets=len(sets), first=first, last=last, wide=wide, weights=weights
    )
    in_specs = [smem()] * 2 + [anywhere()] * len(sets)
    inputs = [plan, new_start, *sets]
    if first:
        in_specs += [anywhere()] * count
        inputs += queries
    else:
        in_specs += [hbm()] * 4
        inputs += [pltpu.with_memory_space_constraint(x, pltpu.HBM) for x in state]
    if weights:
        in_specs += [smem(), anywhere()]
        inputs += [targets, weight]
    if last:
        out_shape = [jax.ShapeDtypeStruct((rows, 128), BF16)] * count
        out_specs = [vmem()] * count
    else:
        out_shape = [pltpu.HBM((count, 128, columns), BF16)]
        out_shape += [pltpu.HBM(s, F32) for s in state_shapes]
        out_specs = [hbm()] * 4
    out_shape += [jax.ShapeDtypeStruct((weight.shape[0], wide), weight.dtype) for _ in range(weights)]
    out_specs += [vmem()] * weights
    states = [pltpu.VMEM(s, F32) for s in state_shapes]
    scratch = [
        pltpu.VMEM((count, 128, columns), BF16),
        pltpu.VMEM((len(sets) * blocks, 128, 128), BF16),
        pltpu.VMEM((len(sets) * blocks, 128, 128), BF16),
        pltpu.VMEM((2, 256, columns), F32),
    ]
    scratch += states + ([pltpu.VMEM((count, 128, columns), BF16)] if first else states)
    scratch += [
        pltpu.SemaphoreType.DMA((2 * len(sets),)),
        pltpu.SemaphoreType.DMA((count + 1,)),
        pltpu.SemaphoreType.DMA((3,)),
        pltpu.SemaphoreType.DMA((2 * max(weights, 1),)),
    ]
    return pl.pallas_call(
        functools.partial(attend_kernel, form),
        out_shape=out_shape,
        in_specs=in_specs,
        out_specs=out_specs,
        scratch_shapes=scratch,
        compiler_params=pltpu.CompilerParams(
            vmem_limit_bytes=LARGE_VMEM_BYTES if weights else VMEM_BYTES
        ),
        cost_estimate=pl.CostEstimate(
            flops=2_000_000_000, bytes_accessed=100_000, transcendentals=0
        ),
        name=name,
    )(*inputs)


def merged(messages, heads, out_ref):
    tails = [m[heads * 128 :, :].astype(F32) for m in messages]
    levels = [t[:heads] + t[heads : 2 * heads] + t[2 * heads : 3 * heads] for t in tails]
    top = functools.reduce(jnp.maximum, levels)
    weights = [jnp.exp2(level - top) for level in levels]
    total = functools.reduce(jnp.add, weights)
    weights = [w / total for w in weights]
    for h in range(heads):
        rows = slice(h * 128, (h + 1) * 128)
        value = sum(m[rows, :].astype(F32) * w[h : h + 1, :] for m, w in zip(messages, weights))
        out_ref[:, rows] = value.T.astype(BF16)


def merge_kernel(heads, *refs):
    merged(refs[:4], heads, refs[4])


def merge(messages, heads):
    return pl.pallas_call(
        functools.partial(merge_kernel, heads),
        out_shape=jax.ShapeDtypeStruct((128, heads * 128), BF16),
        in_specs=[vmem()] * 4,
        out_specs=vmem(),
        compiler_params=pltpu.CompilerParams(vmem_limit_bytes=SMALL_VMEM_BYTES),
        cost_estimate=pl.CostEstimate(flops=2_000_000, bytes_accessed=1_300_000, transcendentals=4096),
        name="merge",
    )(*messages)


def project_kernel(x_ref, w_ref, out_ref):
    out_ref[...] = jnp.dot(x_ref[...], w_ref[...], preferred_element_type=F32).astype(out_ref.dtype)


def project(attended, weight, dtype):
    rows, depth = attended.shape
    wide = weight.shape[1]
    return pl.pallas_call(
        project_kernel,
        out_shape=jax.ShapeDtypeStruct((rows, wide), dtype),
        in_specs=[vmem()] * 2,
        out_specs=vmem(),
        compiler_params=pltpu.CompilerParams(vmem_limit_bytes=SMALL_VMEM_BYTES),
        cost_estimate=pl.CostEstimate(
            flops=2 * rows * depth * wide, bytes_accessed=2 * depth * wide, transcendentals=0
        ),
        name="project",
    )(attended, weight)


def swap(value, axis, mask):
    return lax.ppermute(value, axis, [(i, i ^ mask) for i in range(lax.axis_size(axis))])


def forward(value, axis, by):
    count = lax.axis_size(axis)
    return lax.ppermute(value, axis, [(i, (i + by) % count) for i in range(count)])


def on_device(
    queries,
    incoming_keys,
    incoming_values,
    paged_key_cache,
    paged_value_cache,
    block_table,
    cache_len,
    new_start,
    out_weight,
):
    position = lax.axis_index("ctx")
    column = lax.axis_index("head")
    head_count = lax.axis_size("head")
    blocks = paged_key_cache.shape[0]
    page_size, head_width = paged_key_cache.shape[2:]
    scale = math.log2(math.e) / math.sqrt(head_width)
    wide = out_weight.shape[1] // head_count
    masks = (1, 6, 2, 7, 3, 4, 5)
    me = position.astype(I32).reshape(1)

    def as_blocks(value):
        return value.reshape(-1, page_size, head_width)

    own = jnp.concatenate(
        [as_blocks(v) for v in (paged_key_cache, incoming_keys, paged_value_cache, incoming_values)], axis=0
    )
    far = swap(own, "ctx", 2)
    near = swap(own, "ctx", 1)
    others = [forward(queries, "ctx", 4 * k) for k in range(1, 4)]
    near_own, near_others, far_own, far_others = make_plan(
        me, block_table, cache_len, new_start, blocks, page_size
    )
    state = attend(near_own, new_start, [own, near], scale, queries=[queries], name="attend_near_own")
    near_others, state = lax.optimization_barrier((near_others, state))
    others_state = attend(near_others, new_start, [own, near], scale, queries=others, name="attend_near")
    far, others_state = lax.optimization_barrier((far, others_state))
    far_near = swap(far, "ctx", 1)
    messages = attend(
        far_others, new_start, [far, far_near], scale, state=others_state, last=True, name="attend_far"
    )
    out_weight, far_own, *messages = lax.optimization_barrier([out_weight, far_own, *messages])
    message, *weights = attend(
        far_own, new_start, [far, far_near], scale, state=state, last=True,
        targets=column ^ jnp.array(masks + (0,), I32), weight=out_weight, wide=wide, name="attend_far_own",
    )
    received = [message] + [forward(m, "ctx", -4 * k) for k, m in zip(range(1, 4), messages)]

    attended = merge(received, queries.shape[1] // head_width)
    shares = {}
    for mask, weight, after in zip(masks, weights, (None,) * 5 + masks[:2]):
        given = attended
        if after:
            given, shares[after] = lax.optimization_barrier((attended, shares[after]))
        shares[mask] = swap(project(given, weight, BF16), "head", mask)
    total = project(attended, weights[-1], F32)
    for share in shares.values():
        total = total + share.astype(F32)
    return total.astype(BF16)


def solution(mesh):
    return jax.shard_map(
        on_device,
        mesh=mesh,
        in_specs=(
            P("ctx", "head"),
            P("ctx", "head"),
            P("ctx", "head"),
            P("ctx", "head", None, None),
            P("ctx", "head", None, None),
            P(),
            P(),
            P(),
            P("head", None),
        ),
        out_specs=P("ctx", "head"),
        check_vma=False,
    )
```

```python
import functools
import math

import jax
import jax.numpy as jnp
from jax import lax
from jax.experimental import pallas as pl
from jax.experimental.pallas import tpu as pltpu
from jax.sharding import PartitionSpec as P

F32 = jnp.float32
BF16 = jnp.bfloat16
I32 = jnp.int32

MASKED = -1e30
LOWEST = -1e20
LIST = 64
TASKS = 128
FIELDS = 8
FAR = 1 << 20
VMEM_BYTES = 14 * 1024 * 1024
LARGE_VMEM_BYTES = 30 * 1024 * 1024
SMALL_VMEM_BYTES = 8 * 1024 * 1024


def smem():
    return pl.BlockSpec(memory_space=pltpu.SMEM)


def vmem():
    return pl.BlockSpec(memory_space=pltpu.VMEM)


def anywhere():
    return pl.BlockSpec(memory_space=pl.ANY)


def hbm():
    return pl.BlockSpec(memory_space=pltpu.HBM)


def plan_kernel(requests, blocks, page_size, me_ref, table_ref, len_ref, start_ref, *refs):
    outs, list_ref, count_ref = refs[:4], refs[4], refs[5]
    me = me_ref[0]
    whole_page = page_size * 256

    for r in range(requests):
        length = len_ref[r]
        full = length // page_size
        near_base, far_base = r * LIST, (requests + r) * LIST

        def pages(i, counts, r=r, full=full, near_base=near_base, far_base=far_base):
            near, far = counts
            for u in range(4):
                j = 4 * i + u
                slot = table_ref[r, j]
                relative = (slot >> 4) ^ me
                is_far = relative >= 2
                list_ref[jnp.where(is_far, far, near)] = (
                    (relative & 1) * (blocks + 1) + (slot & 15) + whole_page
                )
                one = jnp.where((relative < 4) & (j < full), 1, 0)
                far_one = jnp.where(is_far, one, 0)
                near, far = near + one - far_one, far + far_one
            return near, far

        near, far = lax.fori_loop(
            0, (full + 3) // 4, pages, (jnp.int32(near_base), jnp.int32(far_base))
        )
        slot = table_ref[r, jnp.minimum(full, table_ref.shape[1] - 1)]
        relative = (slot >> 4) ^ me
        live = length - full * page_size
        is_far = relative >= 2
        list_ref[jnp.where(is_far, far, near)] = (
            (relative & 1) * (blocks + 1) + (slot & 15) + live * 256
        )
        one = jnp.where((relative < 4) & (live > 0), 1, 0)
        far_one = jnp.where(is_far, one, 0)
        count_ref[r] = near + one - far_one
        count_ref[requests + r] = far + far_one

    for out, phase, first_k, last_k in zip(outs, (0, 0, 1, 1), (0, 1, 0, 1), (1, 4, 1, 4)):

        def step(item, first, out=out, phase=phase, first_k=first_k):
            k, r = item // requests + first_k, item % requests
            number = ((me // 4 + 4 - k) % 4) * 4 + me % 4
            low = number * 128
            begin, end = start_ref[r], start_ref[r + 1]

            def add():
                which = phase * requests + r
                base = which * LIST
                total = count_ref[which]
                for side in range(2):
                    other = me ^ (2 * phase + side)
                    list_ref[total] = side * (blocks + 1) + blocks - (1 + other) * 256
                    meets = (other <= number) & (begin < other * 128 + 128) & (end > other * 128)
                    total = total + jnp.where(meets, 1, 0)
                list_ref[total] = 0
                pairs = (total - base + 1) // 2

                def task(i, _):
                    at = (first + i) * FIELDS
                    one, two = list_ref[base + 2 * i], list_ref[base + 2 * i + 1]
                    out[at] = k - first_k
                    out[at + 1] = one
                    out[at + 2] = two
                    out[at + 3] = jnp.where((one >> 8 == page_size) & (two >> 8 == page_size), 0, 1)
                    out[at + 4] = low
                    out[at + 5] = r
                    return 0

                lax.fori_loop(0, pairs, task, 0)
                return first + pairs

            return lax.cond((begin < low + 128) & (end > low), add, lambda: first)

        last = lax.fori_loop(0, (last_k - first_k) * requests, step, jnp.int32(0))
        out[TASKS * FIELDS] = last
        for extra in range(2):
            for field in range(FIELDS):
                out[(last + extra) * FIELDS + field] = 1 if field == 3 else 0


def make_plan(me, block_table, cache_len, new_start, blocks, page_size):
    requests = block_table.shape[0]
    return pl.pallas_call(
        functools.partial(plan_kernel, requests, blocks, page_size),
        out_shape=[pltpu.SMEM((TASKS * FIELDS + 128,), I32)] * 4,
        in_specs=[smem()] * 4,
        out_specs=[smem()] * 4,
        scratch_shapes=[
            pltpu.SMEM((2 * requests * LIST,), I32),
            pltpu.SMEM((2 * requests,), I32),
        ],
        cost_estimate=pl.CostEstimate(flops=1_000_000_000, bytes_accessed=100_000, transcendentals=0),
        name="plan",
    )(me, block_table, cache_len, new_start)


def run_tasks(plan_ref, start_ref, qt_ref, keys_ref, values_ref, scores_ref, acc_ref, high_ref, sum_ref, scale, width, ready):
    columns = qt_ref.shape[2]
    starts = list(range(0, columns, width))

    def place_of(entry):
        return entry & 255

    def score(task, place):
        at = task * FIELDS
        k = plan_ref[at]
        key_block = jnp.concatenate(
            [keys_ref[place_of(plan_ref[at + 1])], keys_ref[place_of(plan_ref[at + 2])]], axis=0
        )
        for c in starts:
            scores_ref[place, :, c : c + width] = jnp.dot(
                key_block, qt_ref[k, :, c : c + width], preferred_element_type=F32
            )

    def absorb(task, place, masked):
        at = task * FIELDS
        k, one, two = plan_ref[at], plan_ref[at + 1], plan_ref[at + 2]
        value_block = jnp.concatenate([values_ref[place_of(one)].T, values_ref[place_of(two)].T], axis=1)
        value_block = jnp.concatenate([value_block, jnp.ones((16, 256), BF16)], axis=0)
        low, r = plan_ref[at + 4], plan_ref[at + 5]
        begin, end = start_ref[r], start_ref[r + 1]
        token = low + lax.broadcasted_iota(I32, (1, width), 1) % 128
        inside = (token >= begin) & (token < end)
        if masked:
            row = lax.broadcasted_iota(I32, (128, 1), 0)
            rows = []
            for entry in (one, two):
                code = entry >> 8
                key = row - (code + 1) * 128
                rows.append(
                    jnp.where(
                        code >= 0,
                        jnp.where(row < code, -1, FAR),
                        jnp.where((key >= begin) & (key < end), key, FAR),
                    )
                )
            key_token = jnp.concatenate(rows, axis=0)
        for c in starts:
            cols = slice(c, c + width)
            scores = scores_ref[place, :, cols]
            if masked:
                scores = jnp.where(key_token <= token, scores, MASKED)
            before = high_ref[k, :, cols]
            high = jnp.where(inside, jnp.maximum(before, jnp.max(scores, axis=0, keepdims=True)), before)
            weights = jnp.exp2(scores * scale - jnp.where(inside, high * scale, -MASKED))
            shrink = jnp.exp2((before - high) * scale)
            part = jnp.dot(value_block, weights.astype(BF16), preferred_element_type=F32)
            high_ref[k, :, cols] = high
            sum_ref[k, :, cols] = sum_ref[k, :, cols] * shrink + part[128:129]
            acc_ref[k, :, cols] = acc_ref[k, :, cols] * shrink + part[:128]

    def step(task, place):
        masked = plan_ref[task * FIELDS + 3]

        @pl.when(masked == 0)
        def _():
            score(task + 1, 1 - place)
            absorb(task, place, False)

        @pl.when(masked != 0)
        def _():
            score(task + 1, 1 - place)
            absorb(task, place, True)

    def two(i, _):
        step(2 * i, 0)
        step(2 * i + 1, 1)
        return 0

    score(0, 0)
    ready()
    lax.fori_loop(0, (plan_ref[TASKS * FIELDS] + 1) // 2, two, 0)


def clear(acc_ref, high_ref, sum_ref):
    acc_ref[...] = jnp.zeros(acc_ref.shape, F32)
    high_ref[...] = jnp.full(high_ref.shape, LOWEST, F32)
    sum_ref[...] = jnp.zeros(sum_ref.shape, F32)


def bring(targets_ref, source_ref, outs, sems, wide):
    pieces = 2
    step = source_ref.shape[0] // pieces
    copies = []
    for n, out in enumerate(outs):
        at = pl.multiple_of(targets_ref[n] * wide, wide)
        for p in range(pieces):
            rows = pl.ds(p * step, step)
            copies.append(
                pltpu.make_async_copy(
                    source_ref.at[rows, pl.ds(at, wide)], out.at[rows], sems.at[n * pieces + p]
                )
            )
            copies[-1].start()
    return copies


def attend_kernel(form, *refs):
    refs = list(refs)

    def take(n):
        taken = refs[:n]
        del refs[:n]
        return taken

    count, blocks, scale = form["count"], form["blocks"], form["scale"]
    first, last, wide, weights = form["first"], form["last"], form["wide"], form["weights"]
    plan_ref, start_ref = take(2)
    sets = take(form["sets"])
    if first:
        query_refs = take(count)
    else:
        qt_in, *state_in = take(4)
    if weights:
        targets_ref, weight_ref = take(2)
    if last:
        message_refs = take(count)
    else:
        qt_out, *state_out = take(4)
    block_refs = take(weights)
    qt_ref, keys_ref, values_ref, scores_ref = take(4)
    state = take(3)
    if first:
        q_ref = take(1)[0]
    else:
        earlier = take(3)
    key_sems, query_sems, state_sems, weight_sems = take(4)
    acc_ref, high_ref, sum_ref = state
    columns = qt_ref.shape[2]
    heads = columns // 128

    queries = []
    if first:
        for k, ref in enumerate(query_refs):
            queries.append(pltpu.make_async_copy(ref, q_ref.at[k], query_sems.at[k]))
    else:
        queries.append(pltpu.make_async_copy(qt_in, qt_ref, query_sems.at[0]))
    key_copies, value_copies, state_copies = [], [], []
    for n, ref in enumerate(sets):
        to = pl.ds(n * blocks, blocks)
        key_copies.append(
            pltpu.make_async_copy(ref.at[pl.ds(0, blocks)], keys_ref.at[to], key_sems.at[2 * n])
        )
        value_copies.append(
            pltpu.make_async_copy(ref.at[pl.ds(blocks, blocks)], values_ref.at[to], key_sems.at[2 * n + 1])
        )
    if not first:
        for n, (source, target) in enumerate(zip(state_in, earlier)):
            state_copies.append(pltpu.make_async_copy(source, target, state_sems.at[n]))
    for copy in queries + key_copies + value_copies + state_copies:
        copy.start()
    brought = bring(targets_ref, weight_ref, block_refs, weight_sems, wide) if weights else []
    clear(acc_ref, high_ref, sum_ref)
    for k, copy in enumerate(queries):
        copy.wait()
        if first:
            for c in range(0, columns, 128):
                qt_ref[k, :, c : c + 128] = q_ref[k, :, c : c + 128].T
    outgoing = []
    if not last:
        outgoing.append(pltpu.make_async_copy(qt_ref, qt_out, query_sems.at[count]))
        outgoing[0].start()
    for copy in key_copies:
        copy.wait()

    def ready():
        for copy in value_copies:
            copy.wait()

    run_tasks(
        plan_ref, start_ref, qt_ref, keys_ref, values_ref, scores_ref, acc_ref, high_ref, sum_ref, scale, 256, ready
    )

    for copy in state_copies:
        copy.wait()
    if not last:
        for n, (source, target) in enumerate(zip(state, state_out)):
            outgoing.append(pltpu.make_async_copy(source, target, state_sems.at[n]))
            outgoing[-1].start()
        for copy in outgoing:
            copy.wait()
        return

    for k in range(count):
        if first:
            high = high_ref[k]
            total = sum_ref[k]
        else:
            acc_a, high_a, sum_a = earlier
            high = jnp.maximum(high_ref[k], high_a[k])
            shrink_a = jnp.exp2((high_a[k] - high) * scale)
            shrink = jnp.exp2((high_ref[k] - high) * scale)
            total = sum_a[k] * shrink_a + sum_ref[k] * shrink
        some = total > 0.0
        safe = jnp.where(some, total, 1.0)
        inverse = jnp.where(some, 1.0 / safe, 0.0)
        level = jnp.where(some, high * scale + jnp.log2(safe), MASKED)
        if not first:
            factor_a, factor = shrink_a * inverse, shrink * inverse
        levels = []
        for h in range(heads):
            cols = slice(h * 128, (h + 1) * 128)
            if first:
                value = acc_ref[k, :, cols] * inverse[:, cols]
            else:
                value = acc_a[k, :, cols] * factor_a[:, cols] + acc_ref[k, :, cols] * factor[:, cols]
            message_refs[k][cols, :] = value.astype(BF16)
            levels.append(level[:, cols])
        level = jnp.concatenate(levels, axis=0)
        one = level.astype(BF16)
        rest = level - one.astype(F32)
        two = rest.astype(BF16)
        three = (rest - two.astype(F32)).astype(BF16)
        tail = jnp.concatenate(
            [one.astype(F32), two.astype(F32), three.astype(F32), jnp.zeros_like(level)], axis=0
        )
        message_refs[k][heads * 128 :, :] = tail.astype(BF16)
    for copy in brought:
        copy.wait()


def attend(plan, new_start, sets, scale, queries=None, state=None, last=False, targets=None, weight=None, wide=0, name="attend"):
    first = state is None
    if first:
        count, columns = len(queries), queries[0].shape[1]
    else:
        count, _, columns = state[0].shape
    blocks = sets[0].shape[0] // 2
    weights = 0 if targets is None else targets.shape[0]
    state_shapes = [(count, 128, columns), (count, 1, columns), (count, 1, columns)]
    rows = columns + 4 * (columns // 128)
    form = dict(
        count=count, blocks=blocks, scale=scale, sets=len(sets), first=first, last=last, wide=wide, weights=weights
    )
    in_specs = [smem()] * 2 + [anywhere()] * len(sets)
    inputs = [plan, new_start, *sets]
    if first:
        in_specs += [anywhere()] * count
        inputs += queries
    else:
        in_specs += [hbm()] * 4
        inputs += [pltpu.with_memory_space_constraint(x, pltpu.HBM) for x in state]
    if weights:
        in_specs += [smem(), anywhere()]
        inputs += [targets, weight]
    if last:
        out_shape = [jax.ShapeDtypeStruct((rows, 128), BF16)] * count
        out_specs = [vmem()] * count
    else:
        out_shape = [pltpu.HBM((count, 128, columns), BF16)]
        out_shape += [pltpu.HBM(s, F32) for s in state_shapes]
        out_specs = [hbm()] * 4
    out_shape += [jax.ShapeDtypeStruct((weight.shape[0], wide), weight.dtype) for _ in range(weights)]
    out_specs += [vmem()] * weights
    states = [pltpu.VMEM(s, F32) for s in state_shapes]
    scratch = [
        pltpu.VMEM((count, 128, columns), BF16),
        pltpu.VMEM((len(sets) * blocks, 128, 128), BF16),
        pltpu.VMEM((len(sets) * blocks, 128, 128), BF16),
        pltpu.VMEM((2, 256, columns), F32),
    ]
    scratch += states + ([pltpu.VMEM((count, 128, columns), BF16)] if first else states)
    scratch += [
        pltpu.SemaphoreType.DMA((2 * len(sets),)),
        pltpu.SemaphoreType.DMA((count + 1,)),
        pltpu.SemaphoreType.DMA((3,)),
        pltpu.SemaphoreType.DMA((2 * max(weights, 1),)),
    ]
    return pl.pallas_call(
        functools.partial(attend_kernel, form),
        out_shape=out_shape,
        in_specs=in_specs,
        out_specs=out_specs,
        scratch_shapes=scratch,
        compiler_params=pltpu.CompilerParams(
            vmem_limit_bytes=LARGE_VMEM_BYTES if weights else VMEM_BYTES
        ),
        cost_estimate=pl.CostEstimate(
            flops=2_000_000_000, bytes_accessed=100_000, transcendentals=0
        ),
        name=name,
    )(*inputs)


def merged(messages, heads, out_ref):
    tails = [m[heads * 128 :, :].astype(F32) for m in messages]
    levels = [t[:heads] + t[heads : 2 * heads] + t[2 * heads : 3 * heads] for t in tails]
    top = functools.reduce(jnp.maximum, levels)
    weights = [jnp.exp2(level - top) for level in levels]
    total = functools.reduce(jnp.add, weights)
    weights = [w / total for w in weights]
    for h in range(heads):
        rows = slice(h * 128, (h + 1) * 128)
        value = sum(m[rows, :].astype(F32) * w[h : h + 1, :] for m, w in zip(messages, weights))
        out_ref[:, rows] = value.T.astype(BF16)


def merge_kernel(heads, *refs):
    merged(refs[:4], heads, refs[4])


def merge(messages, heads):
    return pl.pallas_call(
        functools.partial(merge_kernel, heads),
        out_shape=jax.ShapeDtypeStruct((128, heads * 128), BF16),
        in_specs=[vmem()] * 4,
        out_specs=vmem(),
        compiler_params=pltpu.CompilerParams(vmem_limit_bytes=SMALL_VMEM_BYTES),
        cost_estimate=pl.CostEstimate(flops=2_000_000, bytes_accessed=1_300_000, transcendentals=4096),
        name="merge",
    )(*messages)


def project_kernel(x_ref, w_ref, out_ref):
    out_ref[...] = jnp.dot(x_ref[...], w_ref[...], preferred_element_type=F32).astype(out_ref.dtype)


def project(attended, weight, dtype):
    rows, depth = attended.shape
    wide = weight.shape[1]
    return pl.pallas_call(
        project_kernel,
        out_shape=jax.ShapeDtypeStruct((rows, wide), dtype),
        in_specs=[vmem()] * 2,
        out_specs=vmem(),
        compiler_params=pltpu.CompilerParams(vmem_limit_bytes=SMALL_VMEM_BYTES),
        cost_estimate=pl.CostEstimate(
            flops=2 * rows * depth * wide, bytes_accessed=2 * depth * wide, transcendentals=0
        ),
        name="project",
    )(attended, weight)


def swap(value, axis, mask):
    return lax.ppermute(value, axis, [(i, i ^ mask) for i in range(lax.axis_size(axis))])


def forward(value, axis, by):
    count = lax.axis_size(axis)
    return lax.ppermute(value, axis, [(i, (i + by) % count) for i in range(count)])


def on_device(
    queries,
    incoming_keys,
    incoming_values,
    paged_key_cache,
    paged_value_cache,
    block_table,
    cache_len,
    new_start,
    out_weight,
):
    position = lax.axis_index("ctx")
    column = lax.axis_index("head")
    head_count = lax.axis_size("head")
    blocks = paged_key_cache.shape[0]
    page_size, head_width = paged_key_cache.shape[2:]
    scale = math.log2(math.e) / math.sqrt(head_width)
    wide = out_weight.shape[1] // head_count
    masks = (1, 6, 2, 7, 3, 4, 5)
    me = position.astype(I32).reshape(1)

    def as_blocks(value):
        return value.reshape(-1, page_size, head_width)

    own = jnp.concatenate(
        [as_blocks(v) for v in (paged_key_cache, incoming_keys, paged_value_cache, incoming_values)], axis=0
    )
    far = swap(own, "ctx", 2)
    near = swap(own, "ctx", 1)
    others = [forward(queries, "ctx", 4 * k) for k in range(1, 4)]
    near_own, near_others, far_own, far_others = make_plan(
        me, block_table, cache_len, new_start, blocks, page_size
    )
    state = attend(near_own, new_start, [own, near], scale, queries=[queries], name="attend_near_own")
    near_others, state = lax.optimization_barrier((near_others, state))
    others_state = attend(near_others, new_start, [own, near], scale, queries=others, name="attend_near")
    far, others_state = lax.optimization_barrier((far, others_state))
    far_near = swap(far, "ctx", 1)
    messages = attend(
        far_others, new_start, [far, far_near], scale, state=others_state, last=True, name="attend_far"
    )
    out_weight, far_own, *messages = lax.optimization_barrier([out_weight, far_own, *messages])
    message, *weights = attend(
        far_own, new_start, [far, far_near], scale, state=state, last=True,
        targets=column ^ jnp.array(masks + (0,), I32), weight=out_weight, wide=wide, name="attend_far_own",
    )
    received = [message] + [forward(m, "ctx", -4 * k) for k, m in zip((2, 1, 3), [messages[1], messages[0], messages[2]])]

    attended = merge(received, queries.shape[1] // head_width)
    shares = {}
    for mask, weight, after in zip(masks, weights, (None,) * 5 + masks[:2]):
        given = attended
        if after:
            given, shares[after] = lax.optimization_barrier((attended, shares[after]))
        shares[mask] = swap(project(given, weight, BF16), "head", mask)
    total = project(attended, weights[-1], F32)
    for mask in masks[:5]:
        total = total + shares[mask].astype(F32)
    total = lax.optimization_barrier(total)
    for mask in masks[5:]:
        total = total + shares[mask].astype(F32)
    return total.astype(BF16)


def solution(mesh):
    return jax.shard_map(
        on_device,
        mesh=mesh,
        in_specs=(
            P("ctx", "head"),
            P("ctx", "head"),
            P("ctx", "head"),
            P("ctx", "head", None, None),
            P("ctx", "head", None, None),
            P(),
            P(),
            P(),
            P("head", None),
        ),
        out_specs=P("ctx", "head"),
        check_vma=False,
    )
```

```python
import functools
import math

import jax
import jax.numpy as jnp
from jax import lax
from jax.experimental import pallas as pl
from jax.experimental.pallas import tpu as pltpu
from jax.sharding import PartitionSpec as P

F32 = jnp.float32
BF16 = jnp.bfloat16
I32 = jnp.int32

MASKED = -1e30
LOWEST = -1e20
LIST = 64
TASKS = 128
FIELDS = 8
FAR = 1 << 20
VMEM_BYTES = 14 * 1024 * 1024
LARGE_VMEM_BYTES = 30 * 1024 * 1024
SMALL_VMEM_BYTES = 8 * 1024 * 1024


def smem():
    return pl.BlockSpec(memory_space=pltpu.SMEM)


def vmem():
    return pl.BlockSpec(memory_space=pltpu.VMEM)


def anywhere():
    return pl.BlockSpec(memory_space=pl.ANY)


def hbm():
    return pl.BlockSpec(memory_space=pltpu.HBM)


def plan_kernel(requests, blocks, page_size, me_ref, table_ref, len_ref, start_ref, *refs):
    outs, list_ref, count_ref = refs[:4], refs[4], refs[5]
    me = me_ref[0]
    whole_page = page_size * 256

    for r in range(requests):
        length = len_ref[r]
        full = length // page_size
        near_base, far_base = r * LIST, (requests + r) * LIST

        def pages(i, counts, r=r, full=full, near_base=near_base, far_base=far_base):
            near, far = counts
            for u in range(4):
                j = 4 * i + u
                slot = table_ref[r, j]
                relative = (slot >> 4) ^ me
                is_far = relative >= 2
                list_ref[jnp.where(is_far, far, near)] = (
                    (relative & 1) * (blocks + 1) + (slot & 15) + whole_page
                )
                one = jnp.where((relative < 4) & (j < full), 1, 0)
                far_one = jnp.where(is_far, one, 0)
                near, far = near + one - far_one, far + far_one
            return near, far

        near, far = lax.fori_loop(
            0, (full + 3) // 4, pages, (jnp.int32(near_base), jnp.int32(far_base))
        )
        slot = table_ref[r, jnp.minimum(full, table_ref.shape[1] - 1)]
        relative = (slot >> 4) ^ me
        live = length - full * page_size
        is_far = relative >= 2
        list_ref[jnp.where(is_far, far, near)] = (
            (relative & 1) * (blocks + 1) + (slot & 15) + live * 256
        )
        one = jnp.where((relative < 4) & (live > 0), 1, 0)
        far_one = jnp.where(is_far, one, 0)
        count_ref[r] = near + one - far_one
        count_ref[requests + r] = far + far_one

    for out, phase, first_k, last_k in zip(outs, (0, 0, 1, 1), (0, 1, 0, 1), (1, 4, 1, 4)):

        def step(item, first, out=out, phase=phase, first_k=first_k):
            k, r = item // requests + first_k, item % requests
            number = ((me // 4 + 4 - k) % 4) * 4 + me % 4
            low = number * 128
            begin, end = start_ref[r], start_ref[r + 1]

            def add():
                which = phase * requests + r
                base = which * LIST
                total = count_ref[which]
                for side in range(2):
                    other = me ^ (2 * phase + side)
                    list_ref[total] = side * (blocks + 1) + blocks - (1 + other) * 256
                    meets = (other <= number) & (begin < other * 128 + 128) & (end > other * 128)
                    total = total + jnp.where(meets, 1, 0)
                list_ref[total] = 0
                pairs = (total - base + 1) // 2

                def task(i, _):
                    at = (first + i) * FIELDS
                    one, two = list_ref[base + 2 * i], list_ref[base + 2 * i + 1]
                    out[at] = k - first_k
                    out[at + 1] = one
                    out[at + 2] = two
                    out[at + 3] = jnp.where((one >> 8 == page_size) & (two >> 8 == page_size), 0, 1)
                    out[at + 4] = low
                    out[at + 5] = r
                    return 0

                lax.fori_loop(0, pairs, task, 0)
                return first + pairs

            return lax.cond((begin < low + 128) & (end > low), add, lambda: first)

        last = lax.fori_loop(0, (last_k - first_k) * requests, step, jnp.int32(0))
        out[TASKS * FIELDS] = last
        for extra in range(2):
            for field in range(FIELDS):
                out[(last + extra) * FIELDS + field] = 1 if field == 3 else 0


def make_plan(me, block_table, cache_len, new_start, blocks, page_size):
    requests = block_table.shape[0]
    return pl.pallas_call(
        functools.partial(plan_kernel, requests, blocks, page_size),
        out_shape=[pltpu.SMEM((TASKS * FIELDS + 128,), I32)] * 4,
        in_specs=[smem()] * 4,
        out_specs=[smem()] * 4,
        scratch_shapes=[
            pltpu.SMEM((2 * requests * LIST,), I32),
            pltpu.SMEM((2 * requests,), I32),
        ],
        cost_estimate=pl.CostEstimate(flops=1_000_000_000, bytes_accessed=100_000, transcendentals=0),
        name="plan",
    )(me, block_table, cache_len, new_start)


def run_tasks(plan_ref, start_ref, qt_ref, keys_ref, values_ref, scores_ref, acc_ref, high_ref, sum_ref, scale, width, ready):
    columns = qt_ref.shape[2]
    starts = list(range(0, columns, width))

    def place_of(entry):
        return entry & 255

    def score(task, place):
        at = task * FIELDS
        k = plan_ref[at]
        key_block = jnp.concatenate(
            [keys_ref[place_of(plan_ref[at + 1])], keys_ref[place_of(plan_ref[at + 2])]], axis=0
        )
        for c in starts:
            scores_ref[place, :, c : c + width] = jnp.dot(
                key_block, qt_ref[k, :, c : c + width], preferred_element_type=F32
            )

    def absorb(task, place, masked):
        at = task * FIELDS
        k, one, two = plan_ref[at], plan_ref[at + 1], plan_ref[at + 2]
        value_block = jnp.concatenate([values_ref[place_of(one)].T, values_ref[place_of(two)].T], axis=1)
        value_block = jnp.concatenate([value_block, jnp.ones((16, 256), BF16)], axis=0)
        low, r = plan_ref[at + 4], plan_ref[at + 5]
        begin, end = start_ref[r], start_ref[r + 1]
        token = low + lax.broadcasted_iota(I32, (1, width), 1) % 128
        inside = (token >= begin) & (token < end)
        if masked:
            row = lax.broadcasted_iota(I32, (128, 1), 0)
            rows = []
            for entry in (one, two):
                code = entry >> 8
                key = row - (code + 1) * 128
                rows.append(
                    jnp.where(
                        code >= 0,
                        jnp.where(row < code, -1, FAR),
                        jnp.where((key >= begin) & (key < end), key, FAR),
                    )
                )
            key_token = jnp.concatenate(rows, axis=0)
        for c in starts:
            cols = slice(c, c + width)
            scores = scores_ref[place, :, cols]
            if masked:
                scores = jnp.where(key_token <= token, scores, MASKED)
            before = high_ref[k, :, cols]
            high = jnp.where(inside, jnp.maximum(before, jnp.max(scores, axis=0, keepdims=True)), before)
            weights = jnp.exp2(scores * scale - jnp.where(inside, high * scale, -MASKED))
            shrink = jnp.exp2((before - high) * scale)
            part = jnp.dot(value_block, weights.astype(BF16), preferred_element_type=F32)
            high_ref[k, :, cols] = high
            sum_ref[k, :, cols] = sum_ref[k, :, cols] * shrink + part[128:129]
            acc_ref[k, :, cols] = acc_ref[k, :, cols] * shrink + part[:128]

    def step(task, place):
        masked = plan_ref[task * FIELDS + 3]

        @pl.when(masked == 0)
        def _():
            score(task + 1, 1 - place)
            absorb(task, place, False)

        @pl.when(masked != 0)
        def _():
            score(task + 1, 1 - place)
            absorb(task, place, True)

    def two(i, _):
        step(2 * i, 0)
        step(2 * i + 1, 1)
        return 0

    score(0, 0)
    ready()
    lax.fori_loop(0, (plan_ref[TASKS * FIELDS] + 1) // 2, two, 0)


def clear(acc_ref, high_ref, sum_ref):
    acc_ref[...] = jnp.zeros(acc_ref.shape, F32)
    high_ref[...] = jnp.full(high_ref.shape, LOWEST, F32)
    sum_ref[...] = jnp.zeros(sum_ref.shape, F32)


def bring(targets_ref, source_ref, outs, sems, wide):
    pieces = 2
    step = source_ref.shape[0] // pieces
    copies = []
    for n, out in enumerate(outs):
        at = pl.multiple_of(targets_ref[n] * wide, wide)
        for p in range(pieces):
            rows = pl.ds(p * step, step)
            copies.append(
                pltpu.make_async_copy(
                    source_ref.at[rows, pl.ds(at, wide)], out.at[rows], sems.at[n * pieces + p]
                )
            )
            copies[-1].start()
    return copies


def attend_kernel(form, *refs):
    refs = list(refs)

    def take(n):
        taken = refs[:n]
        del refs[:n]
        return taken

    count, blocks, scale = form["count"], form["blocks"], form["scale"]
    first, last, wide, weights = form["first"], form["last"], form["wide"], form["weights"]
    plan_ref, start_ref = take(2)
    sets = take(form["sets"])
    if first:
        query_refs = take(count)
    else:
        qt_in, *state_in = take(4)
    if weights:
        targets_ref, weight_ref = take(2)
    if last:
        message_refs = take(count)
    else:
        qt_out, *state_out = take(4)
    block_refs = take(weights)
    qt_ref, keys_ref, values_ref, scores_ref = take(4)
    state = take(3)
    if first:
        q_ref = take(1)[0]
    else:
        earlier = take(3)
    key_sems, query_sems, state_sems, weight_sems = take(4)
    acc_ref, high_ref, sum_ref = state
    columns = qt_ref.shape[2]
    heads = columns // 128

    queries = []
    if first:
        for k, ref in enumerate(query_refs):
            queries.append(pltpu.make_async_copy(ref, q_ref.at[k], query_sems.at[k]))
    else:
        queries.append(pltpu.make_async_copy(qt_in, qt_ref, query_sems.at[0]))
    key_copies, value_copies, state_copies = [], [], []
    for n, ref in enumerate(sets):
        to = pl.ds(n * blocks, blocks)
        key_copies.append(
            pltpu.make_async_copy(ref.at[pl.ds(0, blocks)], keys_ref.at[to], key_sems.at[2 * n])
        )
        value_copies.append(
            pltpu.make_async_copy(ref.at[pl.ds(blocks, blocks)], values_ref.at[to], key_sems.at[2 * n + 1])
        )
    if not first:
        for n, (source, target) in enumerate(zip(state_in, earlier)):
            state_copies.append(pltpu.make_async_copy(source, target, state_sems.at[n]))
    for copy in queries + key_copies + value_copies + state_copies:
        copy.start()
    brought = bring(targets_ref, weight_ref, block_refs, weight_sems, wide) if weights else []
    clear(acc_ref, high_ref, sum_ref)
    for k, copy in enumerate(queries):
        copy.wait()
        if first:
            for c in range(0, columns, 128):
                qt_ref[k, :, c : c + 128] = q_ref[k, :, c : c + 128].T
    outgoing = []
    if not last:
        outgoing.append(pltpu.make_async_copy(qt_ref, qt_out, query_sems.at[count]))
        outgoing[0].start()
    for copy in key_copies:
        copy.wait()

    def ready():
        for copy in value_copies:
            copy.wait()

    run_tasks(
        plan_ref, start_ref, qt_ref, keys_ref, values_ref, scores_ref, acc_ref, high_ref, sum_ref, scale, 256, ready
    )

    for copy in state_copies:
        copy.wait()
    if not last:
        for n, (source, target) in enumerate(zip(state, state_out)):
            outgoing.append(pltpu.make_async_copy(source, target, state_sems.at[n]))
            outgoing[-1].start()
        for copy in outgoing:
            copy.wait()
        return

    for k in range(count):
        if first:
            high = high_ref[k]
            total = sum_ref[k]
        else:
            acc_a, high_a, sum_a = earlier
            high = jnp.maximum(high_ref[k], high_a[k])
            shrink_a = jnp.exp2((high_a[k] - high) * scale)
            shrink = jnp.exp2((high_ref[k] - high) * scale)
            total = sum_a[k] * shrink_a + sum_ref[k] * shrink
        some = total > 0.0
        safe = jnp.where(some, total, 1.0)
        inverse = jnp.where(some, 1.0 / safe, 0.0)
        level = jnp.where(some, high * scale + jnp.log2(safe), MASKED)
        if not first:
            factor_a, factor = shrink_a * inverse, shrink * inverse
        levels = []
        for h in range(heads):
            cols = slice(h * 128, (h + 1) * 128)
            if first:
                value = acc_ref[k, :, cols] * inverse[:, cols]
            else:
                value = acc_a[k, :, cols] * factor_a[:, cols] + acc_ref[k, :, cols] * factor[:, cols]
            message_refs[k][cols, :] = value.astype(BF16)
            levels.append(level[:, cols])
        level = jnp.concatenate(levels, axis=0)
        one = level.astype(BF16)
        rest = level - one.astype(F32)
        two = rest.astype(BF16)
        three = (rest - two.astype(F32)).astype(BF16)
        tail = jnp.concatenate(
            [one.astype(F32), two.astype(F32), three.astype(F32), jnp.zeros_like(level)], axis=0
        )
        message_refs[k][heads * 128 :, :] = tail.astype(BF16)
    for copy in brought:
        copy.wait()


def attend(plan, new_start, sets, scale, queries=None, state=None, last=False, targets=None, weight=None, wide=0, name="attend"):
    first = state is None
    if first:
        count, columns = len(queries), queries[0].shape[1]
    else:
        count, _, columns = state[0].shape
    blocks = sets[0].shape[0] // 2
    weights = 0 if targets is None else targets.shape[0]
    state_shapes = [(count, 128, columns), (count, 1, columns), (count, 1, columns)]
    rows = columns + 4 * (columns // 128)
    form = dict(
        count=count, blocks=blocks, scale=scale, sets=len(sets), first=first, last=last, wide=wide, weights=weights
    )
    in_specs = [smem()] * 2 + [anywhere()] * len(sets)
    inputs = [plan, new_start, *sets]
    if first:
        in_specs += [anywhere()] * count
        inputs += queries
    else:
        in_specs += [hbm()] * 4
        inputs += [pltpu.with_memory_space_constraint(x, pltpu.HBM) for x in state]
    if weights:
        in_specs += [smem(), anywhere()]
        inputs += [targets, weight]
    if last:
        out_shape = [jax.ShapeDtypeStruct((rows, 128), BF16)] * count
        out_specs = [vmem()] * count
    else:
        out_shape = [pltpu.HBM((count, 128, columns), BF16)]
        out_shape += [pltpu.HBM(s, F32) for s in state_shapes]
        out_specs = [hbm()] * 4
    out_shape += [jax.ShapeDtypeStruct((weight.shape[0], wide), weight.dtype) for _ in range(weights)]
    out_specs += [vmem()] * weights
    states = [pltpu.VMEM(s, F32) for s in state_shapes]
    scratch = [
        pltpu.VMEM((count, 128, columns), BF16),
        pltpu.VMEM((len(sets) * blocks, 128, 128), BF16),
        pltpu.VMEM((len(sets) * blocks, 128, 128), BF16),
        pltpu.VMEM((2, 256, columns), F32),
    ]
    scratch += states + ([pltpu.VMEM((count, 128, columns), BF16)] if first else states)
    scratch += [
        pltpu.SemaphoreType.DMA((2 * len(sets),)),
        pltpu.SemaphoreType.DMA((count + 1,)),
        pltpu.SemaphoreType.DMA((3,)),
        pltpu.SemaphoreType.DMA((2 * max(weights, 1),)),
    ]
    return pl.pallas_call(
        functools.partial(attend_kernel, form),
        out_shape=out_shape,
        in_specs=in_specs,
        out_specs=out_specs,
        scratch_shapes=scratch,
        compiler_params=pltpu.CompilerParams(
            vmem_limit_bytes=LARGE_VMEM_BYTES if weights else VMEM_BYTES
        ),
        cost_estimate=pl.CostEstimate(
            flops=2_000_000_000, bytes_accessed=100_000, transcendentals=0
        ),
        name=name,
    )(*inputs)


def merged(messages, heads, out_ref):
    tails = [m[heads * 128 :, :].astype(F32) for m in messages]
    levels = [t[:heads] + t[heads : 2 * heads] + t[2 * heads : 3 * heads] for t in tails]
    top = functools.reduce(jnp.maximum, levels)
    weights = [jnp.exp2(level - top) for level in levels]
    total = functools.reduce(jnp.add, weights)
    weights = [w / total for w in weights]
    for h in range(heads):
        rows = slice(h * 128, (h + 1) * 128)
        value = sum(m[rows, :].astype(F32) * w[h : h + 1, :] for m, w in zip(messages, weights))
        out_ref[:, rows] = value.T.astype(BF16)


def merge_kernel(heads, *refs):
    merged(refs[:4], heads, refs[4])


def merge(messages, heads):
    return pl.pallas_call(
        functools.partial(merge_kernel, heads),
        out_shape=jax.ShapeDtypeStruct((128, heads * 128), BF16),
        in_specs=[vmem()] * 4,
        out_specs=vmem(),
        compiler_params=pltpu.CompilerParams(vmem_limit_bytes=SMALL_VMEM_BYTES),
        cost_estimate=pl.CostEstimate(flops=2_000_000, bytes_accessed=1_300_000, transcendentals=4096),
        name="merge",
    )(*messages)


def project_kernel(x_ref, *refs):
    weight_refs, out_ref = refs[:-1], refs[-1]
    wide = weight_refs[0].shape[1]
    for n, w_ref in enumerate(weight_refs):
        out_ref[:, n * wide : (n + 1) * wide] = jnp.dot(
            x_ref[...], w_ref[...], preferred_element_type=F32
        ).astype(out_ref.dtype)


def project(attended, weights, dtype):
    rows, depth = attended.shape
    wide = weights[0].shape[1] * len(weights)
    return pl.pallas_call(
        project_kernel,
        out_shape=jax.ShapeDtypeStruct((rows, wide), dtype),
        in_specs=[vmem()] * (1 + len(weights)),
        out_specs=vmem(),
        compiler_params=pltpu.CompilerParams(vmem_limit_bytes=SMALL_VMEM_BYTES),
        cost_estimate=pl.CostEstimate(
            flops=2 * rows * depth * wide, bytes_accessed=2 * depth * wide, transcendentals=0
        ),
        name="project",
    )(attended, *weights)


def swap(value, axis, mask):
    return lax.ppermute(value, axis, [(i, i ^ mask) for i in range(lax.axis_size(axis))])


def forward(value, axis, by):
    count = lax.axis_size(axis)
    return lax.ppermute(value, axis, [(i, (i + by) % count) for i in range(count)])


def on_device(
    queries,
    incoming_keys,
    incoming_values,
    paged_key_cache,
    paged_value_cache,
    block_table,
    cache_len,
    new_start,
    out_weight,
):
    position = lax.axis_index("ctx")
    column = lax.axis_index("head")
    head_count = lax.axis_size("head")
    blocks = paged_key_cache.shape[0]
    page_size, head_width = paged_key_cache.shape[2:]
    scale = math.log2(math.e) / math.sqrt(head_width)
    wide = out_weight.shape[1] // head_count
    masks = (2, 3, 6, 7, 5, 4, 1)
    me = position.astype(I32).reshape(1)

    def as_blocks(value):
        return value.reshape(-1, page_size, head_width)

    own = jnp.concatenate(
        [as_blocks(v) for v in (paged_key_cache, incoming_keys, paged_value_cache, incoming_values)], axis=0
    )
    far = swap(own, "ctx", 2)
    near = swap(own, "ctx", 1)
    others = [forward(queries, "ctx", 4 * k) for k in range(1, 4)]
    near_own, near_others, far_own, far_others = make_plan(
        me, block_table, cache_len, new_start, blocks, page_size
    )
    state = attend(near_own, new_start, [own, near], scale, queries=[queries], name="attend_near_own")
    near_others, state = lax.optimization_barrier((near_others, state))
    others_state = attend(near_others, new_start, [own, near], scale, queries=others, name="attend_near")
    far, others_state = lax.optimization_barrier((far, others_state))
    far_near = swap(far, "ctx", 1)
    messages = attend(
        far_others, new_start, [far, far_near], scale, state=others_state, last=True, name="attend_far"
    )
    out_weight, far_own, *messages = lax.optimization_barrier([out_weight, far_own, *messages])
    message, *weights = attend(
        far_own, new_start, [far, far_near], scale, state=state, last=True,
        targets=column ^ jnp.array(masks + (0,), I32), weight=out_weight, wide=wide, name="attend_far_own",
    )
    received = [message] + [forward(m, "ctx", -4 * k) for k, m in zip((2, 1, 3), [messages[1], messages[0], messages[2]])]

    attended = merge(received, queries.shape[1] // head_width)
    sides = []
    for n in (0, 2):
        sides.append(swap(project(attended, weights[n : n + 2], BF16), "head", masks[n]))
    across = swap(project(attended, weights[4:5], BF16), "head", 1)
    opposite, cross, total = (project(attended, [w], F32) for w in weights[5:8])
    sides[0], across = lax.optimization_barrier((sides[0], across))
    opposite = swap((opposite + across.astype(F32)).astype(BF16), "head", 4)
    cross = cross + sides[0][:, wide:].astype(F32) + sides[1][:, wide:].astype(F32)
    cross = swap(cross.astype(BF16), "head", 1)
    total = total + sides[0][:, :wide].astype(F32) + sides[1][:, :wide].astype(F32)
    total = lax.optimization_barrier(total)
    total = total + opposite.astype(F32) + cross.astype(F32)
    return total.astype(BF16)


def solution(mesh):
    return jax.shard_map(
        on_device,
        mesh=mesh,
        in_specs=(
            P("ctx", "head"),
            P("ctx", "head"),
            P("ctx", "head"),
            P("ctx", "head", None, None),
            P("ctx", "head", None, None),
            P(),
            P(),
            P(),
            P("head", None),
        ),
        out_specs=P("ctx", "head"),
        check_vma=False,
    )
```

```python
import functools
import math

import jax
import jax.numpy as jnp
from jax import lax
from jax.experimental import pallas as pl
from jax.experimental.pallas import tpu as pltpu
from jax.sharding import PartitionSpec as P

F32 = jnp.float32
BF16 = jnp.bfloat16
I32 = jnp.int32

MASKED = -1e30
LOWEST = -1e20
LIST = 64
TASKS = 128
FIELDS = 8
FAR = 1 << 20
VMEM_BYTES = 14 * 1024 * 1024
LARGE_VMEM_BYTES = 30 * 1024 * 1024
SMALL_VMEM_BYTES = 8 * 1024 * 1024


def smem():
    return pl.BlockSpec(memory_space=pltpu.SMEM)


def vmem():
    return pl.BlockSpec(memory_space=pltpu.VMEM)


def anywhere():
    return pl.BlockSpec(memory_space=pl.ANY)


def hbm():
    return pl.BlockSpec(memory_space=pltpu.HBM)


def plan_kernel(requests, blocks, page_size, me_ref, table_ref, len_ref, start_ref, *refs):
    outs, list_ref, count_ref = refs[:4], refs[4], refs[5]
    me = me_ref[0]
    whole_page = page_size * 256

    for r in range(requests):
        length = len_ref[r]
        full = length // page_size
        near_base, far_base = r * LIST, (requests + r) * LIST

        def pages(i, counts, r=r, full=full, near_base=near_base, far_base=far_base):
            near, far = counts
            for u in range(4):
                j = 4 * i + u
                slot = table_ref[r, j]
                relative = (slot >> 4) ^ me
                is_far = relative >= 2
                list_ref[jnp.where(is_far, far, near)] = (
                    (relative & 1) * (blocks + 1) + (slot & 15) + whole_page
                )
                one = jnp.where((relative < 4) & (j < full), 1, 0)
                far_one = jnp.where(is_far, one, 0)
                near, far = near + one - far_one, far + far_one
            return near, far

        near, far = lax.fori_loop(
            0, (full + 3) // 4, pages, (jnp.int32(near_base), jnp.int32(far_base))
        )
        slot = table_ref[r, jnp.minimum(full, table_ref.shape[1] - 1)]
        relative = (slot >> 4) ^ me
        live = length - full * page_size
        is_far = relative >= 2
        list_ref[jnp.where(is_far, far, near)] = (
            (relative & 1) * (blocks + 1) + (slot & 15) + live * 256
        )
        one = jnp.where((relative < 4) & (live > 0), 1, 0)
        far_one = jnp.where(is_far, one, 0)
        count_ref[r] = near + one - far_one
        count_ref[requests + r] = far + far_one

    for out, phase, first_k, last_k in zip(outs, (0, 0, 1, 1), (0, 1, 0, 1), (1, 4, 1, 4)):

        def step(item, first, out=out, phase=phase, first_k=first_k):
            k, r = item // requests + first_k, item % requests
            number = ((me // 4 + 4 - k) % 4) * 4 + me % 4
            low = number * 128
            begin, end = start_ref[r], start_ref[r + 1]

            def add():
                which = phase * requests + r
                base = which * LIST
                total = count_ref[which]
                for side in range(2):
                    other = me ^ (2 * phase + side)
                    list_ref[total] = side * (blocks + 1) + blocks - (1 + other) * 256
                    meets = (other <= number) & (begin < other * 128 + 128) & (end > other * 128)
                    total = total + jnp.where(meets, 1, 0)
                list_ref[total] = 0
                pairs = (total - base + 1) // 2

                def task(i, _):
                    at = (first + i) * FIELDS
                    one, two = list_ref[base + 2 * i], list_ref[base + 2 * i + 1]
                    out[at] = k - first_k
                    out[at + 1] = one
                    out[at + 2] = two
                    out[at + 3] = jnp.where((one >> 8 == page_size) & (two >> 8 == page_size), 0, 1)
                    out[at + 4] = low
                    out[at + 5] = r
                    return 0

                lax.fori_loop(0, pairs, task, 0)
                return first + pairs

            return lax.cond((begin < low + 128) & (end > low), add, lambda: first)

        last = lax.fori_loop(0, (last_k - first_k) * requests, step, jnp.int32(0))
        out[TASKS * FIELDS] = last
        for extra in range(2):
            for field in range(FIELDS):
                out[(last + extra) * FIELDS + field] = 1 if field == 3 else 0


def make_plan(me, block_table, cache_len, new_start, blocks, page_size):
    requests = block_table.shape[0]
    return pl.pallas_call(
        functools.partial(plan_kernel, requests, blocks, page_size),
        out_shape=[pltpu.SMEM((TASKS * FIELDS + 128,), I32)] * 4,
        in_specs=[smem()] * 4,
        out_specs=[smem()] * 4,
        scratch_shapes=[
            pltpu.SMEM((2 * requests * LIST,), I32),
            pltpu.SMEM((2 * requests,), I32),
        ],
        cost_estimate=pl.CostEstimate(flops=1_000_000_000, bytes_accessed=100_000, transcendentals=0),
        name="plan",
    )(me, block_table, cache_len, new_start)


def run_tasks(plan_ref, start_ref, qt_ref, keys_ref, values_ref, scores_ref, acc_ref, high_ref, sum_ref, scale, width, ready):
    columns = qt_ref.shape[2]
    starts = list(range(0, columns, width))

    def place_of(entry):
        return entry & 255

    def score(task, place):
        at = task * FIELDS
        k = plan_ref[at]
        key_block = jnp.concatenate(
            [keys_ref[place_of(plan_ref[at + 1])], keys_ref[place_of(plan_ref[at + 2])]], axis=0
        )
        for c in starts:
            scores_ref[place, :, c : c + width] = jnp.dot(
                key_block, qt_ref[k, :, c : c + width], preferred_element_type=F32
            )

    def absorb(task, place, masked):
        at = task * FIELDS
        k, one, two = plan_ref[at], plan_ref[at + 1], plan_ref[at + 2]
        value_block = jnp.concatenate([values_ref[place_of(one)].T, values_ref[place_of(two)].T], axis=1)
        value_block = jnp.concatenate([value_block, jnp.ones((16, 256), BF16)], axis=0)
        low, r = plan_ref[at + 4], plan_ref[at + 5]
        begin, end = start_ref[r], start_ref[r + 1]
        token = low + lax.broadcasted_iota(I32, (1, width), 1) % 128
        inside = (token >= begin) & (token < end)
        if masked:
            row = lax.broadcasted_iota(I32, (128, 1), 0)
            rows = []
            for entry in (one, two):
                code = entry >> 8
                key = row - (code + 1) * 128
                rows.append(
                    jnp.where(
                        code >= 0,
                        jnp.where(row < code, -1, FAR),
                        jnp.where((key >= begin) & (key < end), key, FAR),
                    )
                )
            key_token = jnp.concatenate(rows, axis=0)
        for c in starts:
            cols = slice(c, c + width)
            scores = scores_ref[place, :, cols]
            if masked:
                scores = jnp.where(key_token <= token, scores, MASKED)
            before = high_ref[k, :, cols]
            high = jnp.where(inside, jnp.maximum(before, jnp.max(scores, axis=0, keepdims=True)), before)
            weights = jnp.exp2(scores * scale - jnp.where(inside, high * scale, -MASKED))
            shrink = jnp.exp2((before - high) * scale)
            part = jnp.dot(value_block, weights.astype(BF16), preferred_element_type=F32)
            high_ref[k, :, cols] = high
            sum_ref[k, :, cols] = sum_ref[k, :, cols] * shrink + part[128:129]
            acc_ref[k, :, cols] = acc_ref[k, :, cols] * shrink + part[:128]

    def step(task, place):
        masked = plan_ref[task * FIELDS + 3]

        @pl.when(masked == 0)
        def _():
            score(task + 1, 1 - place)
            absorb(task, place, False)

        @pl.when(masked != 0)
        def _():
            score(task + 1, 1 - place)
            absorb(task, place, True)

    def two(i, _):
        step(2 * i, 0)
        step(2 * i + 1, 1)
        return 0

    score(0, 0)
    ready()
    lax.fori_loop(0, (plan_ref[TASKS * FIELDS] + 1) // 2, two, 0)


def clear(acc_ref, high_ref, sum_ref):
    acc_ref[...] = jnp.zeros(acc_ref.shape, F32)
    high_ref[...] = jnp.full(high_ref.shape, LOWEST, F32)
    sum_ref[...] = jnp.zeros(sum_ref.shape, F32)


def bring(targets_ref, source_ref, outs, sems, wide):
    pieces = 2
    step = source_ref.shape[0] // pieces
    copies = []
    for n, out in enumerate(outs):
        at = pl.multiple_of(targets_ref[n] * wide, wide)
        for p in range(pieces):
            rows = pl.ds(p * step, step)
            copies.append(
                pltpu.make_async_copy(
                    source_ref.at[rows, pl.ds(at, wide)], out.at[rows], sems.at[n * pieces + p]
                )
            )
            copies[-1].start()
    return copies


def attend_kernel(form, *refs):
    refs = list(refs)

    def take(n):
        taken = refs[:n]
        del refs[:n]
        return taken

    count, blocks, scale = form["count"], form["blocks"], form["scale"]
    first, last, wide, weights = form["first"], form["last"], form["wide"], form["weights"]
    plan_ref, start_ref = take(2)
    sets = take(form["sets"])
    if first:
        query_refs = take(count)
    else:
        qt_in, *state_in = take(4)
    if weights:
        targets_ref, weight_ref = take(2)
    if last:
        message_refs = take(count)
    else:
        qt_out, *state_out = take(4)
    block_refs = take(weights)
    qt_ref, keys_ref, values_ref, scores_ref = take(4)
    state = take(3)
    if first:
        q_ref = take(1)[0]
    else:
        earlier = take(3)
    key_sems, query_sems, state_sems, weight_sems = take(4)
    acc_ref, high_ref, sum_ref = state
    columns = qt_ref.shape[2]
    heads = columns // 128

    queries = []
    if first:
        for k, ref in enumerate(query_refs):
            queries.append(pltpu.make_async_copy(ref, q_ref.at[k], query_sems.at[k]))
    else:
        queries.append(pltpu.make_async_copy(qt_in, qt_ref, query_sems.at[0]))
    key_copies, value_copies, state_copies = [], [], []
    for n, ref in enumerate(sets):
        to = pl.ds(n * blocks, blocks)
        key_copies.append(
            pltpu.make_async_copy(ref.at[pl.ds(0, blocks)], keys_ref.at[to], key_sems.at[2 * n])
        )
        value_copies.append(
            pltpu.make_async_copy(ref.at[pl.ds(blocks, blocks)], values_ref.at[to], key_sems.at[2 * n + 1])
        )
    if not first:
        for n, (source, target) in enumerate(zip(state_in, earlier)):
            state_copies.append(pltpu.make_async_copy(source, target, state_sems.at[n]))
    for copy in queries + key_copies + value_copies + state_copies:
        copy.start()
    brought = bring(targets_ref, weight_ref, block_refs, weight_sems, wide) if weights else []
    clear(acc_ref, high_ref, sum_ref)
    for k, copy in enumerate(queries):
        copy.wait()
        if first:
            for c in range(0, columns, 128):
                qt_ref[k, :, c : c + 128] = q_ref[k, :, c : c + 128].T
    outgoing = []
    if not last:
        outgoing.append(pltpu.make_async_copy(qt_ref, qt_out, query_sems.at[count]))
        outgoing[0].start()
    for copy in key_copies:
        copy.wait()

    def ready():
        for copy in value_copies:
            copy.wait()

    run_tasks(
        plan_ref, start_ref, qt_ref, keys_ref, values_ref, scores_ref, acc_ref, high_ref, sum_ref, scale, 256, ready
    )

    for copy in state_copies:
        copy.wait()
    if not last:
        for n, (source, target) in enumerate(zip(state, state_out)):
            outgoing.append(pltpu.make_async_copy(source, target, state_sems.at[n]))
            outgoing[-1].start()
        for copy in outgoing:
            copy.wait()
        return

    for k in range(count):
        if first:
            high = high_ref[k]
            total = sum_ref[k]
        else:
            acc_a, high_a, sum_a = earlier
            high = jnp.maximum(high_ref[k], high_a[k])
            shrink_a = jnp.exp2((high_a[k] - high) * scale)
            shrink = jnp.exp2((high_ref[k] - high) * scale)
            total = sum_a[k] * shrink_a + sum_ref[k] * shrink
        some = total > 0.0
        safe = jnp.where(some, total, 1.0)
        inverse = jnp.where(some, 1.0 / safe, 0.0)
        level = jnp.where(some, high * scale + jnp.log2(safe), MASKED)
        if not first:
            factor_a, factor = shrink_a * inverse, shrink * inverse
        levels = []
        for h in range(heads):
            cols = slice(h * 128, (h + 1) * 128)
            if first:
                value = acc_ref[k, :, cols] * inverse[:, cols]
            else:
                value = acc_a[k, :, cols] * factor_a[:, cols] + acc_ref[k, :, cols] * factor[:, cols]
            message_refs[k][cols, :] = value.astype(BF16)
            levels.append(level[:, cols])
        level = jnp.concatenate(levels, axis=0)
        one = level.astype(BF16)
        rest = level - one.astype(F32)
        two = rest.astype(BF16)
        three = (rest - two.astype(F32)).astype(BF16)
        tail = jnp.concatenate(
            [one.astype(F32), two.astype(F32), three.astype(F32), jnp.zeros_like(level)], axis=0
        )
        message_refs[k][heads * 128 :, :] = tail.astype(BF16)
    for copy in brought:
        copy.wait()


def attend(plan, new_start, sets, scale, queries=None, state=None, last=False, targets=None, weight=None, wide=0, name="attend"):
    first = state is None
    if first:
        count, columns = len(queries), queries[0].shape[1]
    else:
        count, _, columns = state[0].shape
    blocks = sets[0].shape[0] // 2
    weights = 0 if targets is None else targets.shape[0]
    state_shapes = [(count, 128, columns), (count, 1, columns), (count, 1, columns)]
    rows = columns + 4 * (columns // 128)
    form = dict(
        count=count, blocks=blocks, scale=scale, sets=len(sets), first=first, last=last, wide=wide, weights=weights
    )
    in_specs = [smem()] * 2 + [anywhere()] * len(sets)
    inputs = [plan, new_start, *sets]
    if first:
        in_specs += [anywhere()] * count
        inputs += queries
    else:
        in_specs += [hbm()] * 4
        inputs += [pltpu.with_memory_space_constraint(x, pltpu.HBM) for x in state]
    if weights:
        in_specs += [smem(), anywhere()]
        inputs += [targets, weight]
    if last:
        out_shape = [jax.ShapeDtypeStruct((rows, 128), BF16)] * count
        out_specs = [vmem()] * count
    else:
        out_shape = [pltpu.HBM((count, 128, columns), BF16)]
        out_shape += [pltpu.HBM(s, F32) for s in state_shapes]
        out_specs = [hbm()] * 4
    out_shape += [jax.ShapeDtypeStruct((weight.shape[0], wide), weight.dtype) for _ in range(weights)]
    out_specs += [vmem()] * weights
    states = [pltpu.VMEM(s, F32) for s in state_shapes]
    scratch = [
        pltpu.VMEM((count, 128, columns), BF16),
        pltpu.VMEM((len(sets) * blocks, 128, 128), BF16),
        pltpu.VMEM((len(sets) * blocks, 128, 128), BF16),
        pltpu.VMEM((2, 256, columns), F32),
    ]
    scratch += states + ([pltpu.VMEM((count, 128, columns), BF16)] if first else states)
    scratch += [
        pltpu.SemaphoreType.DMA((2 * len(sets),)),
        pltpu.SemaphoreType.DMA((count + 1,)),
        pltpu.SemaphoreType.DMA((3,)),
        pltpu.SemaphoreType.DMA((2 * max(weights, 1),)),
    ]
    return pl.pallas_call(
        functools.partial(attend_kernel, form),
        out_shape=out_shape,
        in_specs=in_specs,
        out_specs=out_specs,
        scratch_shapes=scratch,
        compiler_params=pltpu.CompilerParams(
            vmem_limit_bytes=LARGE_VMEM_BYTES if weights else VMEM_BYTES
        ),
        cost_estimate=pl.CostEstimate(
            flops=2_000_000_000, bytes_accessed=100_000, transcendentals=0
        ),
        name=name,
    )(*inputs)


def merged(messages, heads, out_ref):
    tails = [m[heads * 128 :, :].astype(F32) for m in messages]
    levels = [t[:heads] + t[heads : 2 * heads] + t[2 * heads : 3 * heads] for t in tails]
    top = functools.reduce(jnp.maximum, levels)
    weights = [jnp.exp2(level - top) for level in levels]
    total = functools.reduce(jnp.add, weights)
    weights = [w / total for w in weights]
    for h in range(heads):
        rows = slice(h * 128, (h + 1) * 128)
        value = sum(m[rows, :].astype(F32) * w[h : h + 1, :] for m, w in zip(messages, weights))
        out_ref[:, rows] = value.T.astype(BF16)


def merge_kernel(heads, *refs):
    merged(refs[:4], heads, refs[4])


def merge(messages, heads):
    return pl.pallas_call(
        functools.partial(merge_kernel, heads),
        out_shape=jax.ShapeDtypeStruct((128, heads * 128), BF16),
        in_specs=[vmem()] * 4,
        out_specs=vmem(),
        compiler_params=pltpu.CompilerParams(vmem_limit_bytes=SMALL_VMEM_BYTES),
        cost_estimate=pl.CostEstimate(flops=2_000_000, bytes_accessed=1_300_000, transcendentals=4096),
        name="merge",
    )(*messages)


def project_kernel(x_ref, *refs):
    weight_refs, out_ref = refs[:-1], refs[-1]
    wide = weight_refs[0].shape[1]
    for n, w_ref in enumerate(weight_refs):
        out_ref[:, n * wide : (n + 1) * wide] = jnp.dot(
            x_ref[...], w_ref[...], preferred_element_type=F32
        ).astype(out_ref.dtype)


def project(attended, weights, dtype):
    rows, depth = attended.shape
    wide = weights[0].shape[1] * len(weights)
    return pl.pallas_call(
        project_kernel,
        out_shape=jax.ShapeDtypeStruct((rows, wide), dtype),
        in_specs=[vmem()] * (1 + len(weights)),
        out_specs=vmem(),
        compiler_params=pltpu.CompilerParams(vmem_limit_bytes=SMALL_VMEM_BYTES),
        cost_estimate=pl.CostEstimate(
            flops=2 * rows * depth * wide, bytes_accessed=2 * depth * wide, transcendentals=0
        ),
        name="project",
    )(attended, *weights)


def swap(value, axis, mask):
    return lax.ppermute(value, axis, [(i, i ^ mask) for i in range(lax.axis_size(axis))])


def forward(value, axis, by):
    count = lax.axis_size(axis)
    return lax.ppermute(value, axis, [(i, (i + by) % count) for i in range(count)])


def on_device(
    queries,
    incoming_keys,
    incoming_values,
    paged_key_cache,
    paged_value_cache,
    block_table,
    cache_len,
    new_start,
    out_weight,
):
    position = lax.axis_index("ctx")
    column = lax.axis_index("head")
    head_count = lax.axis_size("head")
    blocks = paged_key_cache.shape[0]
    page_size, head_width = paged_key_cache.shape[2:]
    scale = math.log2(math.e) / math.sqrt(head_width)
    wide = out_weight.shape[1] // head_count
    masks = (6, 7, 2, 3, 5, 4, 1)
    me = position.astype(I32).reshape(1)

    def as_blocks(value):
        return value.reshape(-1, page_size, head_width)

    own = jnp.concatenate(
        [as_blocks(v) for v in (paged_key_cache, incoming_keys, paged_value_cache, incoming_values)], axis=0
    )
    far = swap(own, "ctx", 2)
    near = swap(own, "ctx", 1)
    others = [forward(queries, "ctx", 4 * k) for k in range(1, 4)]
    near_own, near_others, far_own, far_others = make_plan(
        me, block_table, cache_len, new_start, blocks, page_size
    )
    state = attend(near_own, new_start, [own, near], scale, queries=[queries], name="attend_near_own")
    near_others, state = lax.optimization_barrier((near_others, state))
    others_state = attend(near_others, new_start, [own, near], scale, queries=others, name="attend_near")
    far, others_state = lax.optimization_barrier((far, others_state))
    far_near = swap(far, "ctx", 1)
    messages = attend(
        far_others, new_start, [far, far_near], scale, state=others_state, last=True, name="attend_far"
    )
    out_weight, far_own, *messages = lax.optimization_barrier([out_weight, far_own, *messages])
    message, *weights = attend(
        far_own, new_start, [far, far_near], scale, state=state, last=True,
        targets=column ^ jnp.array(masks + (0,), I32), weight=out_weight, wide=wide, name="attend_far_own",
    )
    received = [message] + [forward(m, "ctx", -4 * k) for k, m in zip((3, 1, 2), [messages[2], messages[0], messages[1]])]

    attended = merge(received, queries.shape[1] // head_width)
    sides = []
    for n in (0, 2):
        sides.append(swap(project(attended, weights[n : n + 2], BF16), "head", masks[n]))
    across = swap(project(attended, weights[4:5], BF16), "head", 1)
    opposite, cross, total = (project(attended, [w], F32) for w in weights[5:8])
    sides[0], across = lax.optimization_barrier((sides[0], across))
    opposite = swap((opposite + across.astype(F32)).astype(BF16), "head", 4)
    cross = cross + sides[0][:, wide:].astype(F32) + sides[1][:, wide:].astype(F32)
    cross = swap(cross.astype(BF16), "head", 1)
    total = total + sides[0][:, :wide].astype(F32) + sides[1][:, :wide].astype(F32)
    total = lax.optimization_barrier(total)
    total = total + opposite.astype(F32) + cross.astype(F32)
    return total.astype(BF16)


def solution(mesh):
    return jax.shard_map(
        on_device,
        mesh=mesh,
        in_specs=(
            P("ctx", "head"),
            P("ctx", "head"),
            P("ctx", "head"),
            P("ctx", "head", None, None),
            P("ctx", "head", None, None),
            P(),
            P(),
            P(),
            P("head", None),
        ),
        out_specs=P("ctx", "head"),
        check_vma=False,
    )
```

```python
import functools
import math

import jax
import jax.numpy as jnp
from jax import lax
from jax.experimental import pallas as pl
from jax.experimental.pallas import tpu as pltpu
from jax.sharding import PartitionSpec as P

F32 = jnp.float32
BF16 = jnp.bfloat16
I32 = jnp.int32

MASKED = -1e30
LOWEST = -1e20
LIST = 64
TASKS = 128
FIELDS = 8
FAR = 1 << 20
VMEM_BYTES = 14 * 1024 * 1024
LARGE_VMEM_BYTES = 30 * 1024 * 1024
SMALL_VMEM_BYTES = 8 * 1024 * 1024


def smem():
    return pl.BlockSpec(memory_space=pltpu.SMEM)


def vmem():
    return pl.BlockSpec(memory_space=pltpu.VMEM)


def anywhere():
    return pl.BlockSpec(memory_space=pl.ANY)


def hbm():
    return pl.BlockSpec(memory_space=pltpu.HBM)


def plan_kernel(requests, blocks, page_size, me_ref, table_ref, len_ref, start_ref, *refs):
    outs, list_ref, count_ref = refs[:4], refs[4], refs[5]
    me = me_ref[0]
    whole_page = page_size * 256

    for r in range(requests):
        length = len_ref[r]
        full = length // page_size
        near_base, far_base = r * LIST, (requests + r) * LIST

        def pages(i, counts, r=r, full=full, near_base=near_base, far_base=far_base):
            near, far = counts
            for u in range(4):
                j = 4 * i + u
                slot = table_ref[r, j]
                relative = (slot >> 4) ^ me
                is_far = relative >= 2
                list_ref[jnp.where(is_far, far, near)] = (
                    (relative & 1) * (blocks + 1) + (slot & 15) + whole_page
                )
                one = jnp.where((relative < 4) & (j < full), 1, 0)
                far_one = jnp.where(is_far, one, 0)
                near, far = near + one - far_one, far + far_one
            return near, far

        near, far = lax.fori_loop(
            0, (full + 3) // 4, pages, (jnp.int32(near_base), jnp.int32(far_base))
        )
        slot = table_ref[r, jnp.minimum(full, table_ref.shape[1] - 1)]
        relative = (slot >> 4) ^ me
        live = length - full * page_size
        is_far = relative >= 2
        list_ref[jnp.where(is_far, far, near)] = (
            (relative & 1) * (blocks + 1) + (slot & 15) + live * 256
        )
        one = jnp.where((relative < 4) & (live > 0), 1, 0)
        far_one = jnp.where(is_far, one, 0)
        count_ref[r] = near + one - far_one
        count_ref[requests + r] = far + far_one

    for out, phase, first_k, last_k in zip(outs, (0, 0, 1, 1), (0, 1, 0, 1), (1, 4, 1, 4)):

        def step(item, first, out=out, phase=phase, first_k=first_k):
            k, r = item // requests + first_k, item % requests
            number = ((me // 4 + 4 - k) % 4) * 4 + me % 4
            low = number * 128
            begin, end = start_ref[r], start_ref[r + 1]

            def add():
                which = phase * requests + r
                base = which * LIST
                total = count_ref[which]
                for side in range(2):
                    other = me ^ (2 * phase + side)
                    list_ref[total] = side * (blocks + 1) + blocks - (1 + other) * 256
                    meets = (other <= number) & (begin < other * 128 + 128) & (end > other * 128)
                    total = total + jnp.where(meets, 1, 0)
                list_ref[total] = 0
                pairs = (total - base + 1) // 2

                def task(i, _):
                    at = (first + i) * FIELDS
                    one, two = list_ref[base + 2 * i], list_ref[base + 2 * i + 1]
                    out[at] = k - first_k
                    out[at + 1] = one
                    out[at + 2] = two
                    full = (one >> 8 == page_size) & (two >> 8 == page_size)
                    out[at + 3] = jnp.where(two == 0, 2, jnp.where(full, 0, 1))
                    out[at + 4] = low
                    out[at + 5] = r
                    return 0

                lax.fori_loop(0, pairs, task, 0)
                return first + pairs

            return lax.cond((begin < low + 128) & (end > low), add, lambda: first)

        last = lax.fori_loop(0, (last_k - first_k) * requests, step, jnp.int32(0))
        out[TASKS * FIELDS] = last
        for extra in range(2):
            for field in range(FIELDS):
                out[(last + extra) * FIELDS + field] = 1 if field == 3 else 0


def make_plan(me, block_table, cache_len, new_start, blocks, page_size):
    requests = block_table.shape[0]
    return pl.pallas_call(
        functools.partial(plan_kernel, requests, blocks, page_size),
        out_shape=[pltpu.SMEM((TASKS * FIELDS + 128,), I32)] * 4,
        in_specs=[smem()] * 4,
        out_specs=[smem()] * 4,
        scratch_shapes=[
            pltpu.SMEM((2 * requests * LIST,), I32),
            pltpu.SMEM((2 * requests,), I32),
        ],
        cost_estimate=pl.CostEstimate(flops=1_000_000_000, bytes_accessed=100_000, transcendentals=0),
        name="plan",
    )(me, block_table, cache_len, new_start)


def run_tasks(plan_ref, start_ref, qt_ref, keys_ref, values_ref, scores_ref, acc_ref, high_ref, sum_ref, scale, width, ready):
    columns = qt_ref.shape[2]
    starts = list(range(0, columns, width))

    def place_of(entry):
        return entry & 255

    def score(task, place):
        at = task * FIELDS
        k = plan_ref[at]
        key_block = jnp.concatenate(
            [keys_ref[place_of(plan_ref[at + 1])], keys_ref[place_of(plan_ref[at + 2])]], axis=0
        )
        for c in starts:
            scores_ref[place, :, c : c + width] = jnp.dot(
                key_block, qt_ref[k, :, c : c + width], preferred_element_type=F32
            )

    def absorb(task, place, masked, single=False):
        at = task * FIELDS
        k, one, two = plan_ref[at], plan_ref[at + 1], plan_ref[at + 2]
        entries = (one,) if single else (one, two)
        keys = 128 * len(entries)
        value_block = jnp.concatenate([values_ref[place_of(entry)].T for entry in entries], axis=1)
        value_block = jnp.concatenate([value_block, jnp.ones((16, keys), BF16)], axis=0)
        low, r = plan_ref[at + 4], plan_ref[at + 5]
        begin, end = start_ref[r], start_ref[r + 1]
        token = low + lax.broadcasted_iota(I32, (1, width), 1) % 128
        inside = (token >= begin) & (token < end)
        if masked:
            row = lax.broadcasted_iota(I32, (128, 1), 0)
            rows = []
            for entry in entries:
                code = entry >> 8
                key = row - (code + 1) * 128
                rows.append(
                    jnp.where(
                        code >= 0,
                        jnp.where(row < code, -1, FAR),
                        jnp.where((key >= begin) & (key < end), key, FAR),
                    )
                )
            key_token = jnp.concatenate(rows, axis=0)
        for c in starts:
            cols = slice(c, c + width)
            scores = scores_ref[place, :keys, cols]
            if masked:
                scores = jnp.where(key_token <= token, scores, MASKED)
            before = high_ref[k, :, cols]
            high = jnp.where(inside, jnp.maximum(before, jnp.max(scores, axis=0, keepdims=True)), before)
            weights = jnp.exp2(scores * scale - jnp.where(inside, high * scale, -MASKED))
            shrink = jnp.exp2((before - high) * scale)
            part = jnp.dot(value_block, weights.astype(BF16), preferred_element_type=F32)
            high_ref[k, :, cols] = high
            sum_ref[k, :, cols] = sum_ref[k, :, cols] * shrink + part[128:129]
            acc_ref[k, :, cols] = acc_ref[k, :, cols] * shrink + part[:128]

    def step(task, place):
        masked = plan_ref[task * FIELDS + 3]

        @pl.when(masked == 0)
        def _():
            score(task + 1, 1 - place)
            absorb(task, place, False)

        @pl.when(masked == 1)
        def _():
            score(task + 1, 1 - place)
            absorb(task, place, True)

        @pl.when(masked == 2)
        def _():
            score(task + 1, 1 - place)
            absorb(task, place, True, single=True)

    def two(i, _):
        step(2 * i, 0)
        step(2 * i + 1, 1)
        return 0

    score(0, 0)
    ready()
    lax.fori_loop(0, (plan_ref[TASKS * FIELDS] + 1) // 2, two, 0)


def clear(acc_ref, high_ref, sum_ref):
    acc_ref[...] = jnp.zeros(acc_ref.shape, F32)
    high_ref[...] = jnp.full(high_ref.shape, LOWEST, F32)
    sum_ref[...] = jnp.zeros(sum_ref.shape, F32)


def bring(targets_ref, source_ref, outs, sems, wide):
    pieces = 2
    step = source_ref.shape[0] // pieces
    copies = []
    for n, out in enumerate(outs):
        at = pl.multiple_of(targets_ref[n] * wide, wide)
        for p in range(pieces):
            rows = pl.ds(p * step, step)
            copies.append(
                pltpu.make_async_copy(
                    source_ref.at[rows, pl.ds(at, wide)], out.at[rows], sems.at[n * pieces + p]
                )
            )
            copies[-1].start()
    return copies


def attend_kernel(form, *refs):
    refs = list(refs)

    def take(n):
        taken = refs[:n]
        del refs[:n]
        return taken

    count, blocks, scale = form["count"], form["blocks"], form["scale"]
    first, last, wide, weights = form["first"], form["last"], form["wide"], form["weights"]
    plan_ref, start_ref = take(2)
    sets = take(form["sets"])
    if first:
        query_refs = take(count)
    else:
        qt_in, *state_in = take(4)
    if weights:
        targets_ref, weight_ref = take(2)
    if last:
        message_refs = take(count)
    else:
        qt_out, *state_out = take(4)
    block_refs = take(weights)
    qt_ref, keys_ref, values_ref, scores_ref = take(4)
    state = take(3)
    if first:
        q_ref = take(1)[0]
    else:
        earlier = take(3)
    key_sems, query_sems, state_sems, weight_sems = take(4)
    acc_ref, high_ref, sum_ref = state
    columns = qt_ref.shape[2]
    heads = columns // 128

    queries = []
    if first:
        for k, ref in enumerate(query_refs):
            queries.append(pltpu.make_async_copy(ref, q_ref.at[k], query_sems.at[k]))
    else:
        queries.append(pltpu.make_async_copy(qt_in, qt_ref, query_sems.at[0]))
    key_copies, value_copies, state_copies = [], [], []
    for n, ref in enumerate(sets):
        to = pl.ds(n * blocks, blocks)
        key_copies.append(
            pltpu.make_async_copy(ref.at[pl.ds(0, blocks)], keys_ref.at[to], key_sems.at[2 * n])
        )
        value_copies.append(
            pltpu.make_async_copy(ref.at[pl.ds(blocks, blocks)], values_ref.at[to], key_sems.at[2 * n + 1])
        )
    if not first:
        for n, (source, target) in enumerate(zip(state_in, earlier)):
            state_copies.append(pltpu.make_async_copy(source, target, state_sems.at[n]))
    for copy in queries + key_copies + value_copies + state_copies:
        copy.start()
    brought = bring(targets_ref, weight_ref, block_refs, weight_sems, wide) if weights else []
    clear(acc_ref, high_ref, sum_ref)
    for k, copy in enumerate(queries):
        copy.wait()
        if first:
            for c in range(0, columns, 128):
                qt_ref[k, :, c : c + 128] = q_ref[k, :, c : c + 128].T
    outgoing = []
    if not last:
        outgoing.append(pltpu.make_async_copy(qt_ref, qt_out, query_sems.at[count]))
        outgoing[0].start()
    for copy in key_copies:
        copy.wait()

    def ready():
        for copy in value_copies:
            copy.wait()

    run_tasks(
        plan_ref, start_ref, qt_ref, keys_ref, values_ref, scores_ref, acc_ref, high_ref, sum_ref, scale, 256, ready
    )

    for copy in state_copies:
        copy.wait()
    if not last:
        for n, (source, target) in enumerate(zip(state, state_out)):
            outgoing.append(pltpu.make_async_copy(source, target, state_sems.at[n]))
            outgoing[-1].start()
        for copy in outgoing:
            copy.wait()
        return

    for k in range(count):
        if first:
            high = high_ref[k]
            total = sum_ref[k]
        else:
            acc_a, high_a, sum_a = earlier
            high = jnp.maximum(high_ref[k], high_a[k])
            shrink_a = jnp.exp2((high_a[k] - high) * scale)
            shrink = jnp.exp2((high_ref[k] - high) * scale)
            total = sum_a[k] * shrink_a + sum_ref[k] * shrink
        some = total > 0.0
        safe = jnp.where(some, total, 1.0)
        inverse = jnp.where(some, 1.0 / safe, 0.0)
        level = jnp.where(some, high * scale + jnp.log2(safe), MASKED)
        if not first:
            factor_a, factor = shrink_a * inverse, shrink * inverse
        levels = []
        for h in range(heads):
            cols = slice(h * 128, (h + 1) * 128)
            if first:
                value = acc_ref[k, :, cols] * inverse[:, cols]
            else:
                value = acc_a[k, :, cols] * factor_a[:, cols] + acc_ref[k, :, cols] * factor[:, cols]
            message_refs[k][cols, :] = value.astype(BF16)
            levels.append(level[:, cols])
        level = jnp.concatenate(levels, axis=0)
        one = level.astype(BF16)
        rest = level - one.astype(F32)
        two = rest.astype(BF16)
        three = (rest - two.astype(F32)).astype(BF16)
        tail = jnp.concatenate(
            [one.astype(F32), two.astype(F32), three.astype(F32), jnp.zeros_like(level)], axis=0
        )
        message_refs[k][heads * 128 :, :] = tail.astype(BF16)
    for copy in brought:
        copy.wait()


def attend(plan, new_start, sets, scale, queries=None, state=None, last=False, targets=None, weight=None, wide=0, name="attend"):
    first = state is None
    if first:
        count, columns = len(queries), queries[0].shape[1]
    else:
        count, _, columns = state[0].shape
    blocks = sets[0].shape[0] // 2
    weights = 0 if targets is None else targets.shape[0]
    state_shapes = [(count, 128, columns), (count, 1, columns), (count, 1, columns)]
    rows = columns + 4 * (columns // 128)
    form = dict(
        count=count, blocks=blocks, scale=scale, sets=len(sets), first=first, last=last, wide=wide, weights=weights
    )
    in_specs = [smem()] * 2 + [anywhere()] * len(sets)
    inputs = [plan, new_start, *sets]
    if first:
        in_specs += [anywhere()] * count
        inputs += queries
    else:
        in_specs += [hbm()] * 4
        inputs += [pltpu.with_memory_space_constraint(x, pltpu.HBM) for x in state]
    if weights:
        in_specs += [smem(), anywhere()]
        inputs += [targets, weight]
    if last:
        out_shape = [jax.ShapeDtypeStruct((rows, 128), BF16)] * count
        out_specs = [vmem()] * count
    else:
        out_shape = [pltpu.HBM((count, 128, columns), BF16)]
        out_shape += [pltpu.HBM(s, F32) for s in state_shapes]
        out_specs = [hbm()] * 4
    out_shape += [jax.ShapeDtypeStruct((weight.shape[0], wide), weight.dtype) for _ in range(weights)]
    out_specs += [vmem()] * weights
    states = [pltpu.VMEM(s, F32) for s in state_shapes]
    scratch = [
        pltpu.VMEM((count, 128, columns), BF16),
        pltpu.VMEM((len(sets) * blocks, 128, 128), BF16),
        pltpu.VMEM((len(sets) * blocks, 128, 128), BF16),
        pltpu.VMEM((2, 256, columns), F32),
    ]
    scratch += states + ([pltpu.VMEM((count, 128, columns), BF16)] if first else states)
    scratch += [
        pltpu.SemaphoreType.DMA((2 * len(sets),)),
        pltpu.SemaphoreType.DMA((count + 1,)),
        pltpu.SemaphoreType.DMA((3,)),
        pltpu.SemaphoreType.DMA((2 * max(weights, 1),)),
    ]
    return pl.pallas_call(
        functools.partial(attend_kernel, form),
        out_shape=out_shape,
        in_specs=in_specs,
        out_specs=out_specs,
        scratch_shapes=scratch,
        compiler_params=pltpu.CompilerParams(
            vmem_limit_bytes=LARGE_VMEM_BYTES if weights else VMEM_BYTES
        ),
        cost_estimate=pl.CostEstimate(
            flops=2_000_000_000, bytes_accessed=100_000, transcendentals=0
        ),
        name=name,
    )(*inputs)


def merged(messages, heads, out_ref):
    tails = [m[heads * 128 :, :].astype(F32) for m in messages]
    levels = [t[:heads] + t[heads : 2 * heads] + t[2 * heads : 3 * heads] for t in tails]
    top = functools.reduce(jnp.maximum, levels)
    weights = [jnp.exp2(level - top) for level in levels]
    total = functools.reduce(jnp.add, weights)
    weights = [w / total for w in weights]
    for h in range(heads):
        rows = slice(h * 128, (h + 1) * 128)
        value = sum(m[rows, :].astype(F32) * w[h : h + 1, :] for m, w in zip(messages, weights))
        out_ref[:, rows] = value.T.astype(BF16)


def merge_kernel(heads, *refs):
    merged(refs[:4], heads, refs[4])


def merge(messages, heads):
    return pl.pallas_call(
        functools.partial(merge_kernel, heads),
        out_shape=jax.ShapeDtypeStruct((128, heads * 128), BF16),
        in_specs=[vmem()] * 4,
        out_specs=vmem(),
        compiler_params=pltpu.CompilerParams(vmem_limit_bytes=SMALL_VMEM_BYTES),
        cost_estimate=pl.CostEstimate(flops=2_000_000, bytes_accessed=1_300_000, transcendentals=4096),
        name="merge",
    )(*messages)


def project_kernel(x_ref, *refs):
    weight_refs, out_ref = refs[:-1], refs[-1]
    wide = weight_refs[0].shape[1]
    for n, w_ref in enumerate(weight_refs):
        out_ref[:, n * wide : (n + 1) * wide] = jnp.dot(
            x_ref[...], w_ref[...], preferred_element_type=F32
        ).astype(out_ref.dtype)


def project(attended, weights, dtype):
    rows, depth = attended.shape
    wide = weights[0].shape[1] * len(weights)
    return pl.pallas_call(
        project_kernel,
        out_shape=jax.ShapeDtypeStruct((rows, wide), dtype),
        in_specs=[vmem()] * (1 + len(weights)),
        out_specs=vmem(),
        compiler_params=pltpu.CompilerParams(vmem_limit_bytes=SMALL_VMEM_BYTES),
        cost_estimate=pl.CostEstimate(
            flops=2 * rows * depth * wide, bytes_accessed=2 * depth * wide, transcendentals=0
        ),
        name="project",
    )(attended, *weights)


def swap(value, axis, mask):
    return lax.ppermute(value, axis, [(i, i ^ mask) for i in range(lax.axis_size(axis))])


def forward(value, axis, by):
    count = lax.axis_size(axis)
    return lax.ppermute(value, axis, [(i, (i + by) % count) for i in range(count)])


def on_device(
    queries,
    incoming_keys,
    incoming_values,
    paged_key_cache,
    paged_value_cache,
    block_table,
    cache_len,
    new_start,
    out_weight,
):
    position = lax.axis_index("ctx")
    column = lax.axis_index("head")
    head_count = lax.axis_size("head")
    blocks = paged_key_cache.shape[0]
    page_size, head_width = paged_key_cache.shape[2:]
    scale = math.log2(math.e) / math.sqrt(head_width)
    wide = out_weight.shape[1] // head_count
    masks = (6, 7, 2, 3, 5, 4, 1)
    me = position.astype(I32).reshape(1)

    def as_blocks(value):
        return value.reshape(-1, page_size, head_width)

    own = jnp.concatenate(
        [as_blocks(v) for v in (paged_key_cache, incoming_keys, paged_value_cache, incoming_values)], axis=0
    )
    far = swap(own, "ctx", 2)
    near = swap(own, "ctx", 1)
    others = [forward(queries, "ctx", 4 * k) for k in range(1, 4)]
    near_own, near_others, far_own, far_others = make_plan(
        me, block_table, cache_len, new_start, blocks, page_size
    )
    state = attend(near_own, new_start, [own, near], scale, queries=[queries], name="attend_near_own")
    near_others, state = lax.optimization_barrier((near_others, state))
    others_state = attend(near_others, new_start, [own, near], scale, queries=others, name="attend_near")
    far, others_state = lax.optimization_barrier((far, others_state))
    far_near = swap(far, "ctx", 1)
    messages = attend(
        far_others, new_start, [far, far_near], scale, state=others_state, last=True, name="attend_far"
    )
    out_weight, far_own, *messages = lax.optimization_barrier([out_weight, far_own, *messages])
    message, *weights = attend(
        far_own, new_start, [far, far_near], scale, state=state, last=True,
        targets=column ^ jnp.array(masks + (0,), I32), weight=out_weight, wide=wide, name="attend_far_own",
    )
    received = [message] + [forward(m, "ctx", -4 * k) for k, m in zip((3, 1, 2), [messages[2], messages[0], messages[1]])]

    attended = merge(received, queries.shape[1] // head_width)
    sides = []
    for n in (0, 2):
        sides.append(swap(project(attended, weights[n : n + 2], BF16), "head", masks[n]))
    across = swap(project(attended, weights[4:5], BF16), "head", 1)
    opposite, cross, total = (project(attended, [w], F32) for w in weights[5:8])
    sides[0], across = lax.optimization_barrier((sides[0], across))
    opposite = swap((opposite + across.astype(F32)).astype(BF16), "head", 4)
    cross = cross + sides[0][:, wide:].astype(F32) + sides[1][:, wide:].astype(F32)
    cross = swap(cross.astype(BF16), "head", 1)
    total = total + sides[0][:, :wide].astype(F32) + sides[1][:, :wide].astype(F32)
    total = lax.optimization_barrier(total)
    total = total + opposite.astype(F32) + cross.astype(F32)
    return total.astype(BF16)


def solution(mesh):
    return jax.shard_map(
        on_device,
        mesh=mesh,
        in_specs=(
            P("ctx", "head"),
            P("ctx", "head"),
            P("ctx", "head"),
            P("ctx", "head", None, None),
            P("ctx", "head", None, None),
            P(),
            P(),
            P(),
            P("head", None),
        ),
        out_specs=P("ctx", "head"),
        check_vma=False,
    )
```

```python
import functools
import math

import jax
import jax.numpy as jnp
from jax import lax
from jax.experimental import pallas as pl
from jax.experimental.pallas import tpu as pltpu
from jax.sharding import PartitionSpec as P

F32 = jnp.float32
BF16 = jnp.bfloat16
I32 = jnp.int32

MASKED = -1e30
LOWEST = -1e20
LIST = 64
TASKS = 128
FIELDS = 8
FAR = 1 << 20
VMEM_BYTES = 14 * 1024 * 1024
LARGE_VMEM_BYTES = 30 * 1024 * 1024
SMALL_VMEM_BYTES = 8 * 1024 * 1024


def smem():
    return pl.BlockSpec(memory_space=pltpu.SMEM)


def vmem():
    return pl.BlockSpec(memory_space=pltpu.VMEM)


def anywhere():
    return pl.BlockSpec(memory_space=pl.ANY)


def hbm():
    return pl.BlockSpec(memory_space=pltpu.HBM)


def plan_kernel(requests, blocks, page_size, me_ref, table_ref, len_ref, start_ref, *refs):
    outs, list_ref, count_ref = refs[:4], refs[4], refs[5]
    me = me_ref[0]
    whole_page = page_size * 256

    for r in range(requests):
        length = len_ref[r]
        full = length // page_size
        near_base, far_base = r * LIST, (requests + r) * LIST

        def pages(i, counts, r=r, full=full, near_base=near_base, far_base=far_base):
            near, far = counts
            for u in range(4):
                j = 4 * i + u
                slot = table_ref[r, j]
                relative = (slot >> 4) ^ me
                is_far = relative >= 2
                list_ref[jnp.where(is_far, far, near)] = (
                    (relative & 1) * (blocks + 1) + (slot & 15) + whole_page
                )
                one = jnp.where((relative < 4) & (j < full), 1, 0)
                far_one = jnp.where(is_far, one, 0)
                near, far = near + one - far_one, far + far_one
            return near, far

        near, far = lax.fori_loop(
            0, (full + 3) // 4, pages, (jnp.int32(near_base), jnp.int32(far_base))
        )
        slot = table_ref[r, jnp.minimum(full, table_ref.shape[1] - 1)]
        relative = (slot >> 4) ^ me
        live = length - full * page_size
        is_far = relative >= 2
        list_ref[jnp.where(is_far, far, near)] = (
            (relative & 1) * (blocks + 1) + (slot & 15) + live * 256
        )
        one = jnp.where((relative < 4) & (live > 0), 1, 0)
        far_one = jnp.where(is_far, one, 0)
        count_ref[r] = near + one - far_one
        count_ref[requests + r] = far + far_one

    for out, phase, first_k, last_k in zip(outs, (0, 0, 1, 1), (0, 1, 0, 1), (1, 4, 1, 4)):

        def step(item, first, out=out, phase=phase, first_k=first_k):
            k, r = item // requests + first_k, item % requests
            number = ((me // 4 + 4 - k) % 4) * 4 + me % 4
            low = number * 128
            begin, end = start_ref[r], start_ref[r + 1]

            def add():
                which = phase * requests + r
                base = which * LIST
                total = count_ref[which]
                for side in range(2):
                    other = me ^ (2 * phase + side)
                    list_ref[total] = side * (blocks + 1) + blocks - (1 + other) * 256
                    meets = (other <= number) & (begin < other * 128 + 128) & (end > other * 128)
                    total = total + jnp.where(meets, 1, 0)
                list_ref[total] = 0
                pairs = (total - base + 1) // 2

                def task(i, _):
                    at = (first + i) * FIELDS
                    one, two = list_ref[base + 2 * i], list_ref[base + 2 * i + 1]
                    out[at] = k - first_k
                    out[at + 1] = one
                    out[at + 2] = two
                    full = (one >> 8 == page_size) & (two >> 8 == page_size)
                    alone = jnp.where(one >> 8 == page_size, 2, 3)
                    out[at + 3] = jnp.where(two == 0, alone, jnp.where(full, 0, 1))
                    out[at + 4] = low
                    out[at + 5] = r
                    return 0

                lax.fori_loop(0, pairs, task, 0)
                return first + pairs

            return lax.cond((begin < low + 128) & (end > low), add, lambda: first)

        last = lax.fori_loop(0, (last_k - first_k) * requests, step, jnp.int32(0))
        out[TASKS * FIELDS] = last
        for extra in range(2):
            for field in range(FIELDS):
                out[(last + extra) * FIELDS + field] = 1 if field == 3 else 0


def make_plan(me, block_table, cache_len, new_start, blocks, page_size):
    requests = block_table.shape[0]
    return pl.pallas_call(
        functools.partial(plan_kernel, requests, blocks, page_size),
        out_shape=[pltpu.SMEM((TASKS * FIELDS + 128,), I32)] * 4,
        in_specs=[smem()] * 4,
        out_specs=[smem()] * 4,
        scratch_shapes=[
            pltpu.SMEM((2 * requests * LIST,), I32),
            pltpu.SMEM((2 * requests,), I32),
        ],
        cost_estimate=pl.CostEstimate(flops=1_000_000_000, bytes_accessed=100_000, transcendentals=0),
        name="plan",
    )(me, block_table, cache_len, new_start)


def run_tasks(plan_ref, start_ref, qt_ref, keys_ref, values_ref, scores_ref, acc_ref, high_ref, sum_ref, scale, width, ready):
    columns = qt_ref.shape[2]
    starts = list(range(0, columns, width))

    def place_of(entry):
        return entry & 255

    def score(task, place):
        at = task * FIELDS
        k = plan_ref[at]
        key_block = jnp.concatenate(
            [keys_ref[place_of(plan_ref[at + 1])], keys_ref[place_of(plan_ref[at + 2])]], axis=0
        )
        for c in starts:
            scores_ref[place, :, c : c + width] = jnp.dot(
                key_block, qt_ref[k, :, c : c + width], preferred_element_type=F32
            )

    def absorb(task, place, masked, single=False):
        at = task * FIELDS
        k, one, two = plan_ref[at], plan_ref[at + 1], plan_ref[at + 2]
        entries = (one,) if single else (one, two)
        keys = 128 * len(entries)
        value_block = jnp.concatenate([values_ref[place_of(entry)].T for entry in entries], axis=1)
        value_block = jnp.concatenate([value_block, jnp.ones((16, keys), BF16)], axis=0)
        low, r = plan_ref[at + 4], plan_ref[at + 5]
        begin, end = start_ref[r], start_ref[r + 1]
        token = low + lax.broadcasted_iota(I32, (1, width), 1) % 128
        inside = (token >= begin) & (token < end)
        if masked:
            row = lax.broadcasted_iota(I32, (128, 1), 0)
            rows = []
            for entry in entries:
                code = entry >> 8
                key = row - (code + 1) * 128
                rows.append(
                    jnp.where(
                        code >= 0,
                        jnp.where(row < code, -1, FAR),
                        jnp.where((key >= begin) & (key < end), key, FAR),
                    )
                )
            key_token = jnp.concatenate(rows, axis=0)
        for c in starts:
            cols = slice(c, c + width)
            scores = scores_ref[place, :keys, cols]
            if masked:
                scores = jnp.where(key_token <= token, scores, MASKED)
            before = high_ref[k, :, cols]
            high = jnp.where(inside, jnp.maximum(before, jnp.max(scores, axis=0, keepdims=True)), before)
            weights = jnp.exp2(scores * scale - jnp.where(inside, high * scale, -MASKED))
            shrink = jnp.exp2((before - high) * scale)
            part = jnp.dot(value_block, weights.astype(BF16), preferred_element_type=F32)
            high_ref[k, :, cols] = high
            sum_ref[k, :, cols] = sum_ref[k, :, cols] * shrink + part[128:129]
            acc_ref[k, :, cols] = acc_ref[k, :, cols] * shrink + part[:128]

    def step(task, place):
        masked = plan_ref[task * FIELDS + 3]

        @pl.when(masked == 0)
        def _():
            score(task + 1, 1 - place)
            absorb(task, place, False)

        @pl.when(masked == 1)
        def _():
            score(task + 1, 1 - place)
            absorb(task, place, True)

        @pl.when(masked == 2)
        def _():
            score(task + 1, 1 - place)
            absorb(task, place, False, single=True)

        @pl.when(masked == 3)
        def _():
            score(task + 1, 1 - place)
            absorb(task, place, True, single=True)

    def two(i, _):
        step(2 * i, 0)
        step(2 * i + 1, 1)
        return 0

    score(0, 0)
    ready()
    lax.fori_loop(0, (plan_ref[TASKS * FIELDS] + 1) // 2, two, 0)


def clear(acc_ref, high_ref, sum_ref):
    acc_ref[...] = jnp.zeros(acc_ref.shape, F32)
    high_ref[...] = jnp.full(high_ref.shape, LOWEST, F32)
    sum_ref[...] = jnp.zeros(sum_ref.shape, F32)


def bring(targets_ref, source_ref, outs, sems, wide):
    pieces = 2
    step = source_ref.shape[0] // pieces
    copies = []
    for n, out in enumerate(outs):
        at = pl.multiple_of(targets_ref[n] * wide, wide)
        for p in range(pieces):
            rows = pl.ds(p * step, step)
            copies.append(
                pltpu.make_async_copy(
                    source_ref.at[rows, pl.ds(at, wide)], out.at[rows], sems.at[n * pieces + p]
                )
            )
            copies[-1].start()
    return copies


def attend_kernel(form, *refs):
    refs = list(refs)

    def take(n):
        taken = refs[:n]
        del refs[:n]
        return taken

    count, blocks, scale = form["count"], form["blocks"], form["scale"]
    first, last, wide, weights = form["first"], form["last"], form["wide"], form["weights"]
    plan_ref, start_ref = take(2)
    sets = take(form["sets"])
    if first:
        query_refs = take(count)
    else:
        qt_in, *state_in = take(4)
    if weights:
        targets_ref, weight_ref = take(2)
    if last:
        message_refs = take(count)
    else:
        qt_out, *state_out = take(4)
    block_refs = take(weights)
    qt_ref, keys_ref, values_ref, scores_ref = take(4)
    state = take(3)
    if first:
        q_ref = take(1)[0]
    else:
        earlier = take(3)
    key_sems, query_sems, state_sems, weight_sems = take(4)
    acc_ref, high_ref, sum_ref = state
    columns = qt_ref.shape[2]
    heads = columns // 128

    queries = []
    if first:
        for k, ref in enumerate(query_refs):
            queries.append(pltpu.make_async_copy(ref, q_ref.at[k], query_sems.at[k]))
    else:
        queries.append(pltpu.make_async_copy(qt_in, qt_ref, query_sems.at[0]))
    key_copies, value_copies, state_copies = [], [], []
    for n, ref in enumerate(sets):
        to = pl.ds(n * blocks, blocks)
        key_copies.append(
            pltpu.make_async_copy(ref.at[pl.ds(0, blocks)], keys_ref.at[to], key_sems.at[2 * n])
        )
        value_copies.append(
            pltpu.make_async_copy(ref.at[pl.ds(blocks, blocks)], values_ref.at[to], key_sems.at[2 * n + 1])
        )
    if not first:
        for n, (source, target) in enumerate(zip(state_in, earlier)):
            state_copies.append(pltpu.make_async_copy(source, target, state_sems.at[n]))
    for copy in queries + key_copies + value_copies + state_copies:
        copy.start()
    brought = bring(targets_ref, weight_ref, block_refs, weight_sems, wide) if weights else []
    clear(acc_ref, high_ref, sum_ref)
    for k, copy in enumerate(queries):
        copy.wait()
        if first:
            for c in range(0, columns, 128):
                qt_ref[k, :, c : c + 128] = q_ref[k, :, c : c + 128].T
    outgoing = []
    if not last:
        outgoing.append(pltpu.make_async_copy(qt_ref, qt_out, query_sems.at[count]))
        outgoing[0].start()
    for copy in key_copies:
        copy.wait()

    def ready():
        for copy in value_copies:
            copy.wait()

    run_tasks(
        plan_ref, start_ref, qt_ref, keys_ref, values_ref, scores_ref, acc_ref, high_ref, sum_ref, scale, 256, ready
    )

    for copy in state_copies:
        copy.wait()
    if not last:
        for n, (source, target) in enumerate(zip(state, state_out)):
            outgoing.append(pltpu.make_async_copy(source, target, state_sems.at[n]))
            outgoing[-1].start()
        for copy in outgoing:
            copy.wait()
        return

    for k in range(count):
        if first:
            high = high_ref[k]
            total = sum_ref[k]
        else:
            acc_a, high_a, sum_a = earlier
            high = jnp.maximum(high_ref[k], high_a[k])
            shrink_a = jnp.exp2((high_a[k] - high) * scale)
            shrink = jnp.exp2((high_ref[k] - high) * scale)
            total = sum_a[k] * shrink_a + sum_ref[k] * shrink
        some = total > 0.0
        safe = jnp.where(some, total, 1.0)
        inverse = jnp.where(some, 1.0 / safe, 0.0)
        level = jnp.where(some, high * scale + jnp.log2(safe), MASKED)
        if not first:
            factor_a, factor = shrink_a * inverse, shrink * inverse
        levels = []
        for h in range(heads):
            cols = slice(h * 128, (h + 1) * 128)
            if first:
                value = acc_ref[k, :, cols] * inverse[:, cols]
            else:
                value = acc_a[k, :, cols] * factor_a[:, cols] + acc_ref[k, :, cols] * factor[:, cols]
            message_refs[k][cols, :] = value.astype(BF16)
            levels.append(level[:, cols])
        level = jnp.concatenate(levels, axis=0)
        one = level.astype(BF16)
        rest = level - one.astype(F32)
        two = rest.astype(BF16)
        three = (rest - two.astype(F32)).astype(BF16)
        tail = jnp.concatenate(
            [one.astype(F32), two.astype(F32), three.astype(F32), jnp.zeros_like(level)], axis=0
        )
        message_refs[k][heads * 128 :, :] = tail.astype(BF16)
    for copy in brought:
        copy.wait()


def attend(plan, new_start, sets, scale, queries=None, state=None, last=False, targets=None, weight=None, wide=0, name="attend"):
    first = state is None
    if first:
        count, columns = len(queries), queries[0].shape[1]
    else:
        count, _, columns = state[0].shape
    blocks = sets[0].shape[0] // 2
    weights = 0 if targets is None else targets.shape[0]
    state_shapes = [(count, 128, columns), (count, 1, columns), (count, 1, columns)]
    rows = columns + 4 * (columns // 128)
    form = dict(
        count=count, blocks=blocks, scale=scale, sets=len(sets), first=first, last=last, wide=wide, weights=weights
    )
    in_specs = [smem()] * 2 + [anywhere()] * len(sets)
    inputs = [plan, new_start, *sets]
    if first:
        in_specs += [anywhere()] * count
        inputs += queries
    else:
        in_specs += [hbm()] * 4
        inputs += [pltpu.with_memory_space_constraint(x, pltpu.HBM) for x in state]
    if weights:
        in_specs += [smem(), anywhere()]
        inputs += [targets, weight]
    if last:
        out_shape = [jax.ShapeDtypeStruct((rows, 128), BF16)] * count
        out_specs = [vmem()] * count
    else:
        out_shape = [pltpu.HBM((count, 128, columns), BF16)]
        out_shape += [pltpu.HBM(s, F32) for s in state_shapes]
        out_specs = [hbm()] * 4
    out_shape += [jax.ShapeDtypeStruct((weight.shape[0], wide), weight.dtype) for _ in range(weights)]
    out_specs += [vmem()] * weights
    states = [pltpu.VMEM(s, F32) for s in state_shapes]
    scratch = [
        pltpu.VMEM((count, 128, columns), BF16),
        pltpu.VMEM((len(sets) * blocks, 128, 128), BF16),
        pltpu.VMEM((len(sets) * blocks, 128, 128), BF16),
        pltpu.VMEM((2, 256, columns), F32),
    ]
    scratch += states + ([pltpu.VMEM((count, 128, columns), BF16)] if first else states)
    scratch += [
        pltpu.SemaphoreType.DMA((2 * len(sets),)),
        pltpu.SemaphoreType.DMA((count + 1,)),
        pltpu.SemaphoreType.DMA((3,)),
        pltpu.SemaphoreType.DMA((2 * max(weights, 1),)),
    ]
    return pl.pallas_call(
        functools.partial(attend_kernel, form),
        out_shape=out_shape,
        in_specs=in_specs,
        out_specs=out_specs,
        scratch_shapes=scratch,
        compiler_params=pltpu.CompilerParams(
            vmem_limit_bytes=LARGE_VMEM_BYTES if weights else VMEM_BYTES
        ),
        cost_estimate=pl.CostEstimate(
            flops=2_000_000_000, bytes_accessed=100_000, transcendentals=0
        ),
        name=name,
    )(*inputs)


def merged(messages, heads, out_ref):
    tails = [m[heads * 128 :, :].astype(F32) for m in messages]
    levels = [t[:heads] + t[heads : 2 * heads] + t[2 * heads : 3 * heads] for t in tails]
    top = functools.reduce(jnp.maximum, levels)
    weights = [jnp.exp2(level - top) for level in levels]
    total = functools.reduce(jnp.add, weights)
    weights = [w / total for w in weights]
    for h in range(heads):
        rows = slice(h * 128, (h + 1) * 128)
        value = sum(m[rows, :].astype(F32) * w[h : h + 1, :] for m, w in zip(messages, weights))
        out_ref[:, rows] = value.T.astype(BF16)


def merge_kernel(heads, *refs):
    merged(refs[:4], heads, refs[4])


def merge(messages, heads):
    return pl.pallas_call(
        functools.partial(merge_kernel, heads),
        out_shape=jax.ShapeDtypeStruct((128, heads * 128), BF16),
        in_specs=[vmem()] * 4,
        out_specs=vmem(),
        compiler_params=pltpu.CompilerParams(vmem_limit_bytes=SMALL_VMEM_BYTES),
        cost_estimate=pl.CostEstimate(flops=2_000_000, bytes_accessed=1_300_000, transcendentals=4096),
        name="merge",
    )(*messages)


def project_kernel(x_ref, *refs):
    weight_refs, out_ref = refs[:-1], refs[-1]
    wide = weight_refs[0].shape[1]
    for n, w_ref in enumerate(weight_refs):
        out_ref[:, n * wide : (n + 1) * wide] = jnp.dot(
            x_ref[...], w_ref[...], preferred_element_type=F32
        ).astype(out_ref.dtype)


def project(attended, weights, dtype):
    rows, depth = attended.shape
    wide = weights[0].shape[1] * len(weights)
    return pl.pallas_call(
        project_kernel,
        out_shape=jax.ShapeDtypeStruct((rows, wide), dtype),
        in_specs=[vmem()] * (1 + len(weights)),
        out_specs=vmem(),
        compiler_params=pltpu.CompilerParams(vmem_limit_bytes=SMALL_VMEM_BYTES),
        cost_estimate=pl.CostEstimate(
            flops=2 * rows * depth * wide, bytes_accessed=2 * depth * wide, transcendentals=0
        ),
        name="project",
    )(attended, *weights)


def swap(value, axis, mask):
    return lax.ppermute(value, axis, [(i, i ^ mask) for i in range(lax.axis_size(axis))])


def forward(value, axis, by):
    count = lax.axis_size(axis)
    return lax.ppermute(value, axis, [(i, (i + by) % count) for i in range(count)])


def on_device(
    queries,
    incoming_keys,
    incoming_values,
    paged_key_cache,
    paged_value_cache,
    block_table,
    cache_len,
    new_start,
    out_weight,
):
    position = lax.axis_index("ctx")
    column = lax.axis_index("head")
    head_count = lax.axis_size("head")
    blocks = paged_key_cache.shape[0]
    page_size, head_width = paged_key_cache.shape[2:]
    scale = math.log2(math.e) / math.sqrt(head_width)
    wide = out_weight.shape[1] // head_count
    masks = (6, 7, 2, 3, 5, 4, 1)
    me = position.astype(I32).reshape(1)

    def as_blocks(value):
        return value.reshape(-1, page_size, head_width)

    own = jnp.concatenate(
        [as_blocks(v) for v in (paged_key_cache, incoming_keys, paged_value_cache, incoming_values)], axis=0
    )
    far = swap(own, "ctx", 2)
    near = swap(own, "ctx", 1)
    others = [forward(queries, "ctx", 4 * k) for k in range(1, 4)]
    near_own, near_others, far_own, far_others = make_plan(
        me, block_table, cache_len, new_start, blocks, page_size
    )
    state = attend(near_own, new_start, [own, near], scale, queries=[queries], name="attend_near_own")
    near_others, state = lax.optimization_barrier((near_others, state))
    others_state = attend(near_others, new_start, [own, near], scale, queries=others, name="attend_near")
    far, others_state = lax.optimization_barrier((far, others_state))
    far_near = swap(far, "ctx", 1)
    messages = attend(
        far_others, new_start, [far, far_near], scale, state=others_state, last=True, name="attend_far"
    )
    out_weight, far_own, *messages = lax.optimization_barrier([out_weight, far_own, *messages])
    message, *weights = attend(
        far_own, new_start, [far, far_near], scale, state=state, last=True,
        targets=column ^ jnp.array(masks + (0,), I32), weight=out_weight, wide=wide, name="attend_far_own",
    )
    received = [message] + [forward(m, "ctx", -4 * k) for k, m in zip((3, 1, 2), [messages[2], messages[0], messages[1]])]

    attended = merge(received, queries.shape[1] // head_width)
    sides = []
    for n in (0, 2):
        sides.append(swap(project(attended, weights[n : n + 2], BF16), "head", masks[n]))
    across = swap(project(attended, weights[4:5], BF16), "head", 1)
    opposite, cross, total = (project(attended, [w], F32) for w in weights[5:8])
    sides[0], across = lax.optimization_barrier((sides[0], across))
    opposite = swap((opposite + across.astype(F32)).astype(BF16), "head", 4)
    cross = cross + sides[0][:, wide:].astype(F32) + sides[1][:, wide:].astype(F32)
    cross = swap(cross.astype(BF16), "head", 1)
    total = total + sides[0][:, :wide].astype(F32) + sides[1][:, :wide].astype(F32)
    total = lax.optimization_barrier(total)
    total = total + opposite.astype(F32) + cross.astype(F32)
    return total.astype(BF16)


def solution(mesh):
    return jax.shard_map(
        on_device,
        mesh=mesh,
        in_specs=(
            P("ctx", "head"),
            P("ctx", "head"),
            P("ctx", "head"),
            P("ctx", "head", None, None),
            P("ctx", "head", None, None),
            P(),
            P(),
            P(),
            P("head", None),
        ),
        out_specs=P("ctx", "head"),
        check_vma=False,
    )
```
